128 devices in a mesh: row: 16 (over y, z_lo, core), col: 8 (over z_hi, x).
Axes of the slice: x: 4, y: 4, z: 4 (z_hi: 2, z_lo: 2; z = z_hi * 2 + z_lo), core: 2. Of those that a mesh axis runs over, the one named last changes fastest.
Arguments:
- kv_cache: bfloat16 [256, 128, 2, 1536], P('row', 'col'), may hold values from -20 to 20
- fresh_qkv: bfloat16 [256, 128, 3, 1536], P('row', 'col'), may hold values from -20 to 20
- edit_list: int32 [4, 8], P(None, 'col'), may hold values from 0 to 16, as said below
Outputs:
- attended: bfloat16 [256, 128, 1536], P('row', 'col')
The draws below stay inside these ranges and needn't reach their ends.
Inputs may be any that keep to these rules, and one draw needn't show every extreme that they name: `edit_list`: each column lists its distinct edited tile rows in increasing order, at least one, then 16 in the unused entries; some column lists 4 rows.
All inputs are finite; a program needn't handle non-finite values.
Results may differ from the reference program's by a relative error of at most 0.017.
Values may be sent and summed in bfloat16 or wider, within the bound.
No kernel may reach another device: no remote copies, remote signals or barrier semaphores. Data moves between devices by JAX's collectives and lax.ppermute only.
A program may use at most 256 MiB of HBM per device.

```python
import math
import jax
import jax.numpy as jnp
from jax import lax

TILE = 16
HEADS = 12
DEPTH = 128
F = 1536
COL_MOST = 4
NH = 256
NW = 128
N_ROW = 16
N_COL = 8


def planted_layout(key):
    key = jax.random.fold_in(key, 101)
    head_key, coord_key, sign_key, band_key, peak_key, spot_key = jax.random.split(key, 6)
    planted_count = max(1, HEADS // 2)
    head_order = jax.random.permutation(head_key, HEADS)
    head_flags = head_order < planted_count
    support = max(1, DEPTH // 8)
    coord_orders = jax.vmap(lambda one_key: jax.random.permutation(one_key, DEPTH))(jax.random.split(coord_key, HEADS))
    coord_flags = coord_orders < support
    signs = (2 * jax.random.randint(sign_key, (HEADS, DEPTH), 0, 2) - 1).astype(jnp.float32)
    spread = math.sqrt(math.sqrt(DEPTH) / support)
    pattern = jnp.where(coord_flags, signs * spread, 0.0).astype(jnp.float32).reshape(F)
    heavy_band = jax.random.randint(band_key, (), 0, N_ROW)
    peak_band = (heavy_band + jax.random.randint(peak_key, (), 1, N_ROW)) % N_ROW
    peak_row = peak_band * TILE + jax.random.randint(spot_key, (), 0, TILE)
    peak_col = 4 % NW
    token_rows = jnp.arange(NH) // TILE
    in_heavy = token_rows == heavy_band
    row_level = jnp.where(in_heavy, 4.0, 3.0).astype(jnp.float32)
    level = jnp.broadcast_to(row_level[:, None], (NH, NW))
    peak_spot = (jnp.arange(NH)[:, None] == peak_row) & (jnp.arange(NW)[None, :] == peak_col)
    level = jnp.where(peak_spot, 6.5, level).astype(jnp.float32)
    offset = jnp.broadcast_to(jnp.where(in_heavy, 2.5, 0.0).astype(jnp.float32)[:, None], (NH, NW))
    head_mask = jnp.repeat(head_flags, DEPTH)
    coord_mask = coord_flags.reshape(F)
    return (head_mask, coord_mask, pattern, level, offset)


def planted_keys(rough_keys, level, pattern, coord_mask):
    noise_scale = jnp.where(coord_mask, 0.2, 1.5).astype(jnp.float32)
    return level[:, :, None] * pattern[None, None, :] + rough_keys * noise_scale[None, None, :]


def drawn_values(rough_values, offset):
    return offset[:, :, None] + 1.5 * rough_values


def build_cache(rough, layout):
    head_mask, coord_mask, pattern, level, offset = layout
    keys_part = planted_keys(rough[:, :, 0, :], level, pattern, coord_mask)
    values_part = drawn_values(rough[:, :, 1, :], offset)
    planted = jnp.stack([keys_part, values_part], axis=2)
    mixed = jnp.where(head_mask[None, None, None, :], planted, 3.0 * rough)
    return jnp.clip(mixed, -19.5, 19.5)


def draw_kv_cache(key, part):
    layout = planted_layout(key)
    key = jax.random.fold_in(key, 7)
    rough = jnp.clip(jax.random.normal(key, (NH, NW, 2, F), jnp.float32), -5.0, 5.0)
    mixed = build_cache(rough, layout)
    return mixed.astype(jnp.bfloat16)


def build_fresh(rough, reach, layout):
    head_mask, coord_mask, pattern, level, offset = layout
    channel_scale = jnp.array([1.0, 3.0, 3.0], jnp.float32)[None, None, :, None]
    base = rough * channel_scale
    queries_part = reach[:, :, None] * pattern[None, None, :] + 0.2 * rough[:, :, 0, :]
    keys_part = planted_keys(rough[:, :, 1, :], level, pattern, coord_mask)
    values_part = drawn_values(rough[:, :, 2, :], offset)
    planted = jnp.stack([queries_part, keys_part, values_part], axis=2)
    return jnp.where(head_mask[None, None, None, :], planted, base)


def draw_fresh_qkv(key, part):
    layout = planted_layout(key)
    key = jax.random.fold_in(key, 11)
    first_key = jax.random.fold_in(key, 0)
    third_key = jax.random.fold_in(key, 2)
    reach = jax.random.uniform(third_key, (NH, NW), jnp.float32, 2.0, 4.4)
    rough = jnp.clip(jax.random.normal(first_key, (NH, NW, 3, F), jnp.float32), -5.0, 5.0)
    mixed = build_fresh(rough, reach, layout)
    return jnp.clip(mixed, -19.5, 19.5).astype(jnp.bfloat16)


def draw_edit_list(key, part):
    key = jax.random.fold_in(key, 5)
    count_key, full_key, order_key = jax.random.split(key, 3)
    counts = jax.random.randint(count_key, (N_COL,), 1, max(2, COL_MOST // 2 + 1))
    full_column = jax.random.randint(full_key, (), 0, N_COL)
    counts = jnp.where(jnp.arange(N_COL) == full_column, COL_MOST, counts)
    orders = jax.vmap(lambda column_key: jax.random.permutation(column_key, N_ROW))(jax.random.split(order_key, N_COL))
    chosen = orders[:, :COL_MOST]
    slot_ids = jnp.arange(COL_MOST)
    listed = jnp.where(slot_ids[None, :] < counts[:, None], chosen, N_ROW)
    listed = jnp.sort(listed, axis=1)
    return listed.T.astype(jnp.int32)


def setup_inputs(seed: int = 0) -> dict:
    arg_keys = jax.random.split(jax.random.key(seed), 4)
    kv_cache = draw_kv_cache(jax.random.fold_in(arg_keys[3], 71), 0)
    fresh_qkv = draw_fresh_qkv(jax.random.fold_in(arg_keys[3], 71), 0)
    edit_list = draw_edit_list(jax.random.fold_in(arg_keys[3], 71), 0)
    return dict(kv_cache=kv_cache, fresh_qkv=fresh_qkv, edit_list=edit_list)


def tile_attention(query_tile, key_heads, value_heads, head_size):
    query_heads = query_tile.reshape(query_tile.shape[0], -1, head_size).transpose(1, 0, 2)
    score_scale = 1.0 / math.sqrt(head_size)

    def one_head(operands):
        query_one, key_one, value_one = operands
        scores = jnp.dot(query_one, key_one.T, preferred_element_type=jnp.float32) * score_scale
        row_max = lax.optimization_barrier(jnp.max(scores, axis=1, keepdims=True))
        weights = jnp.exp(scores - row_max)
        row_total = lax.optimization_barrier(jnp.sum(weights, axis=1, keepdims=True))
        numerator = jnp.dot(weights.astype(jnp.bfloat16), value_one, preferred_element_type=jnp.float32)
        return numerator / row_total
    outputs = lax.map(one_head, (query_heads, key_heads, value_heads))
    return outputs.transpose(1, 0, 2).reshape(query_tile.shape[0], -1).astype(jnp.bfloat16)

def reference(kv_cache, fresh_qkv, edit_list):
    tile_rows = jnp.arange(N_ROW, dtype=jnp.int32)
    hits = edit_list[:, None, :] == tile_rows[None, :, None]
    edit_flags = jnp.any(hits, axis=0)
    token_flags = jnp.repeat(jnp.repeat(edit_flags, TILE, axis=0), TILE, axis=1)
    merged = jnp.where(token_flags[:, :, None, None], fresh_qkv[:, :, 1:, :], kv_cache)
    merged = merged.reshape(NH * NW, 2, F)
    key_heads = merged[:, 0, :].reshape(NH * NW, HEADS, DEPTH).transpose(1, 0, 2)
    value_heads = merged[:, 1, :].reshape(NH * NW, HEADS, DEPTH).transpose(1, 0, 2)
    query_tiles = fresh_qkv[:, :, 0, :].reshape(N_ROW, TILE, N_COL, TILE, F).transpose(0, 2, 1, 3, 4)
    safe_rows = jnp.minimum(edit_list, N_ROW - 1).astype(jnp.int32)
    column_ids = jnp.arange(N_COL, dtype=jnp.int32)
    picked = query_tiles[safe_rows, column_ids[None, :]]
    picked = picked.reshape(COL_MOST * N_COL, TILE * TILE, F)
    results = lax.map(lambda query_tile: tile_attention(query_tile, key_heads, value_heads, DEPTH), picked)
    results = results.reshape(COL_MOST, N_COL, TILE * TILE, F).astype(jnp.float32)
    placed = jnp.einsum('jrc,jctf->rctf', hits.astype(jnp.float32), results)
    placed = placed.reshape(N_ROW, N_COL, TILE, TILE, F).transpose(0, 2, 1, 3, 4).reshape(NH, NW, F)
    return placed.astype(jnp.bfloat16)
```

```python
import math

import jax
import jax.numpy as jnp
from jax import lax
from jax.experimental import pallas as pl
from jax.experimental.pallas import tpu as pltpu
from jax.sharding import Mesh, PartitionSpec as P

DEPTH = 128
SLOTS = 4
TOKS = 256
HALF = 128
QUART = 64
KV_ROWS = 4 * HALF
Q_ROWS = HALF + QUART
MSG_ROWS = KV_ROWS + Q_ROWS
SLOT_ROWS = Q_ROWS + 16
GROUP = 4
KEY_BLOCK = 512
MIB = 1024 * 1024


def vmem():
    return pl.BlockSpec(memory_space=pltpu.VMEM)


def smem():
    return pl.BlockSpec(memory_space=pltpu.SMEM)


def pack_kernel(q_ref, k_ref, v_ref, out_ref):
    for chip in range(2):
        full = slice(0, DEPTH) if chip == 0 else slice(2 * DEPTH, 3 * DEPTH)
        shared = slice(DEPTH, 2 * DEPTH)
        for core in range(2):
            dest = chip * 2 + core
            toks = slice(core * HALF, (core + 1) * HALF)
            quart = slice(core * HALF + chip * QUART, core * HALF + (chip + 1) * QUART)
            out_ref[dest, 0:HALF, :] = k_ref[toks, full]
            out_ref[dest, HALF : 2 * HALF, :] = v_ref[toks, full]
            out_ref[dest, 2 * HALF : 3 * HALF, :] = k_ref[toks, shared]
            out_ref[dest, 3 * HALF : 4 * HALF, :] = v_ref[toks, shared]
            out_ref[dest, KV_ROWS : KV_ROWS + HALF, :] = q_ref[toks, full]
            out_ref[dest, KV_ROWS + HALF : MSG_ROWS, :] = q_ref[quart, shared]


def pack(query, keys, values):
    spec = pl.BlockSpec((TOKS, 3 * DEPTH), lambda p: (0, p))
    return pl.pallas_call(
        pack_kernel,
        grid=(4,),
        in_specs=[spec] * 3,
        out_specs=pl.BlockSpec((4, MSG_ROWS, DEPTH), lambda p: (p, 0, 0)),
        out_shape=jax.ShapeDtypeStruct((16, MSG_ROWS, DEPTH), jnp.bfloat16),
    )(query, keys, values)


def attend_rows(queries, k_refs, kv_refs, head, vext):
    fold = math.log2(math.e) / math.sqrt(DEPTH)
    row_max = None
    acc = None
    blocks = 2048 // KEY_BLOCK
    tiles = KEY_BLOCK // HALF
    first = 2 * HALF * head
    for part in range(2):
        for block in range(blocks):
            rows = slice(block * tiles, (block + 1) * tiles)
            keys = kv_refs[part][rows, first : first + HALF, :].reshape(KEY_BLOCK, DEPTH)
            scores = (
                lax.dot_general(
                    queries, keys, (((1,), (1,)), ((), ())), preferred_element_type=jnp.float32
                )
                * fold
            )
            block_max = jnp.max(scores, axis=1, keepdims=True)
            new_max = block_max if row_max is None else jnp.maximum(row_max, block_max)
            weights = jnp.exp2(scores - new_max).astype(jnp.bfloat16)
            start = part * 2048 + block * KEY_BLOCK
            term = jnp.dot(
                weights,
                vext[head, start : start + KEY_BLOCK, :],
                preferred_element_type=jnp.float32,
            )
            if row_max is None:
                acc = term
            else:
                acc = acc * jnp.exp2(row_max - new_max) + term
            row_max = new_max
    total = acc[:, DEPTH:]
    out = (acc[:, :DEPTH] / total).astype(jnp.bfloat16)
    return out, jnp.log2(total) + row_max


def attend_kernel(valid_ref, q_ref, own_ref, other_ref, out_ref, vext, table):
    slots = q_ref.shape[0]
    for head in range(2):
        first = 2 * HALF * head + HALF
        vext[head, 0:2048, 0:DEPTH] = own_ref[:, first : first + HALF, :].reshape(2048, DEPTH)
        vext[head, 2048:4096, 0:DEPTH] = other_ref[:, first : first + HALF, :].reshape(2048, DEPTH)
        vext[head, :, DEPTH:] = jnp.ones((4096, DEPTH), jnp.bfloat16)

    def note(slot, count):
        is_valid = valid_ref[slot]

        @pl.when(is_valid == 1)
        def _():
            table[count] = slot

        return count + is_valid

    count = lax.fori_loop(0, slots, note, jnp.int32(0))
    for extra in range(GROUP):
        table[count + extra] = table[0]

    kv_refs = (own_ref, other_ref)

    def body(group, carry):
        picks = [table[group * GROUP + i] for i in range(GROUP)]
        full = jnp.concatenate([q_ref[pick, 0:HALF, :] for pick in picks], axis=0)
        out_full, lse_full = attend_rows(full, None, kv_refs, 0, vext)
        shared = jnp.concatenate([q_ref[pick, HALF:Q_ROWS, :] for pick in picks], axis=0)
        out_shared, lse_shared = attend_rows(shared, None, kv_refs, 1, vext)
        row_ids = lax.broadcasted_iota(jnp.int32, (16, DEPTH), 0)
        for i, pick in enumerate(picks):
            out_ref[pick, 0:HALF, :] = out_full[i * HALF : (i + 1) * HALF]
            out_ref[pick, HALF:Q_ROWS, :] = out_shared[i * QUART : (i + 1) * QUART]
            lse_one = lse_shared[i * QUART : (i + 1) * QUART]
            pair = (
                jnp.transpose(lse_full[i * HALF : (i + 1) * HALF]),
                jnp.transpose(jnp.concatenate([lse_one, lse_one], axis=0)),
            )
            stats = jnp.zeros((16, DEPTH), jnp.float32)
            for j, lanes in enumerate(pair):
                rest = lanes[0:16]
                for term in range(3):
                    piece = rest.astype(jnp.bfloat16).astype(jnp.float32)
                    rest = rest - piece
                    stats = jnp.where(row_ids == 3 * j + term, piece, stats)
            out_ref[pick, Q_ROWS:SLOT_ROWS, :] = stats.astype(jnp.bfloat16)
        return carry

    lax.fori_loop(0, pl.cdiv(count, GROUP), body, 0)


def attend(valid, queries, own, other):
    slots = queries.shape[0]
    return pl.pallas_call(
        attend_kernel,
        in_specs=[smem(), vmem(), vmem(), vmem()],
        out_specs=vmem(),
        out_shape=jax.ShapeDtypeStruct((slots, SLOT_ROWS, DEPTH), jnp.bfloat16),
        scratch_shapes=[
            pltpu.VMEM((2, 4096, 2 * DEPTH), jnp.bfloat16),
            pltpu.SMEM((slots + GROUP,), jnp.int32),
        ],
        compiler_params=pltpu.CompilerParams(vmem_limit_bytes=48 * MIB),
    )(valid, queries, own, other)


def combine_kernel(rows_ref, part_ref, out_ref):
    out_ref[...] = jnp.zeros_like(out_ref)
    band_count = out_ref.shape[0]
    sources = part_ref.shape[0]
    for slot in range(SLOTS):
        row = rows_ref[slot]

        @pl.when(row < band_count)
        def _():
            stats = [
                part_ref[i, slot, Q_ROWS:SLOT_ROWS, :].astype(jnp.float32) for i in range(sources)
            ]
            for j, (first, size) in enumerate(((0, HALF), (HALF, QUART))):
                lses = [s[3 * j : 3 * j + 1] + s[3 * j + 1 : 3 * j + 2] + s[3 * j + 2 : 3 * j + 3] for s in stats]
                top = lses[0]
                for lse in lses[1:]:
                    top = jnp.maximum(top, lse)
                shares = [jnp.exp2(lse - top) for lse in lses]
                whole = shares[0]
                for share in shares[1:]:
                    whole = whole + share
                total = jnp.zeros((size, DEPTH), jnp.float32)
                for i in range(sources):
                    share = jnp.broadcast_to(shares[i] / whole, (DEPTH, DEPTH))
                    total = total + jnp.transpose(share)[0:size] * part_ref[
                        i, slot, first : first + size, :
                    ].astype(jnp.float32)
                out_ref[row, first : first + size, :] = total.astype(jnp.bfloat16)


def combine(listed_rows, partials, band_count):
    return pl.pallas_call(
        combine_kernel,
        in_specs=[smem(), vmem()],
        out_specs=vmem(),
        out_shape=jax.ShapeDtypeStruct((band_count, Q_ROWS, DEPTH), jnp.bfloat16),
        compiler_params=pltpu.CompilerParams(vmem_limit_bytes=24 * MIB),
    )(listed_rows, partials)


def unpack_kernel(in_ref, out_ref):
    for chip in range(2):
        full = slice(0, DEPTH) if chip == 0 else slice(2 * DEPTH, 3 * DEPTH)
        for core in range(2):
            source = chip * 2 + core
            first = core * HALF + chip * QUART
            out_ref[core * HALF : (core + 1) * HALF, full] = in_ref[source, 0:HALF, :]
            out_ref[first : first + QUART, DEPTH : 2 * DEPTH] = in_ref[source, HALF:Q_ROWS, :]


def unpack(received, features):
    return pl.pallas_call(
        unpack_kernel,
        grid=(4,),
        in_specs=[pl.BlockSpec((4, Q_ROWS, DEPTH), lambda p: (p, 0, 0))],
        out_specs=pl.BlockSpec((TOKS, 3 * DEPTH), lambda p: (0, p)),
        out_shape=jax.ShapeDtypeStruct((TOKS, features), jnp.bfloat16),
    )(received)


def per_device(kv_cache, fresh_qkv, edit_list):
    tile_edge, tile_width, _, features = kv_cache.shape
    row_axes = ("chip", "core")
    band_count = lax.axis_size(row_axes)
    col_count = lax.axis_size("col")
    my_row = lax.axis_index(row_axes)
    listed_rows = edit_list[:, 0]
    own_edited = jnp.any(listed_rows == my_row)
    keys = jnp.where(own_edited, fresh_qkv[:, :, 1, :], kv_cache[:, :, 0, :])
    values = jnp.where(own_edited, fresh_qkv[:, :, 2, :], kv_cache[:, :, 1, :])
    query = fresh_qkv[:, :, 0, :]
    flat = (TOKS, features)
    message = pack(query.reshape(flat), keys.reshape(flat), values.reshape(flat))
    received = lax.all_to_all(message, row_axes, 0, 0, tiled=True)
    other = lax.ppermute(received[:, :KV_ROWS], "core", [(0, 1), (1, 0)])

    safe_rows = jnp.minimum(listed_rows, band_count - 1)
    picked = jnp.stack(
        [
            lax.dynamic_slice(received, (safe_rows[s], KV_ROWS, 0), (1, Q_ROWS, DEPTH))[0]
            for s in range(SLOTS)
        ]
    )
    flags = (listed_rows < band_count).astype(jnp.bfloat16)
    heads = jnp.broadcast_to(flags[:, None, None], (SLOTS, 16, DEPTH))
    mine = jnp.concatenate([picked, heads], axis=1)
    spread = jnp.broadcast_to(mine[None], (col_count,) + mine.shape)
    queries = lax.all_to_all(spread, "col", 0, 0, tiled=True)
    queries = queries.reshape(col_count * SLOTS, SLOT_ROWS, DEPTH)
    valid = queries[:, Q_ROWS, 0].astype(jnp.int32)

    partials = attend(valid, queries, received, other)
    partials = partials.reshape(col_count, SLOTS, SLOT_ROWS, DEPTH)
    partials = lax.all_to_all(partials, "col", 0, 0, tiled=True)
    finished = combine(listed_rows, partials, band_count)
    finished = lax.all_to_all(finished, row_axes, 0, 0, tiled=True)
    return unpack(finished, features).reshape(tile_edge, tile_width, features)


def solution(mesh):
    rows, cols = mesh.devices.shape
    fine = Mesh(mesh.devices.reshape(rows // 2, 2, cols), ("chip", "core", "col"))
    split = ("chip", "core")
    placed = (P(split, "col", None, None), P(split, "col", None, None), P(None, "col"))
    return jax.shard_map(
        per_device, mesh=fine, in_specs=placed, out_specs=P(split, "col", None), check_vma=False
    )
```

```python
import functools
import math

import jax
import jax.numpy as jnp
from jax import lax
from jax.experimental import pallas as pl
from jax.experimental.pallas import tpu as pltpu
from jax.sharding import Mesh, PartitionSpec as P

DEPTH = 128
SLOTS = 4
TOKS = 256
HALF = 128
QUART = 64
KV_ROWS = 4 * HALF
Q_ROWS = HALF + QUART
MSG_ROWS = KV_ROWS + Q_ROWS
SLOT_ROWS = Q_ROWS + 16
GROUP = 4
KEY_BLOCK = 512
MIB = 1024 * 1024


def vmem():
    return pl.BlockSpec(memory_space=pltpu.VMEM)


def smem():
    return pl.BlockSpec(memory_space=pltpu.SMEM)


def cost(flops, moved):
    return pl.CostEstimate(flops=flops, bytes_accessed=moved, transcendentals=0)


def fresh_spec(part):
    return pl.BlockSpec((16, 1, 16, 3 * DEPTH), lambda p: (0, part, 0, p))


def pack_kernel(row_axes, rows_ref, cache_ref, query_ref, keys_ref, values_ref, out_ref):
    my_row = lax.axis_index(row_axes)
    edited = rows_ref[0] == my_row
    for slot in range(1, SLOTS):
        edited = jnp.logical_or(edited, rows_ref[slot] == my_row)

    def place(core, head, keys, values):
        for chip in ((0,), (0, 1), (1,))[head]:
            first = 2 * HALF if head == 1 else 0
            out_ref[chip * 2 + core, first : first + HALF, :] = keys
            out_ref[chip * 2 + core, first + HALF : first + 2 * HALF, :] = values

    for chip in range(2):
        full = slice(0, DEPTH) if chip == 0 else slice(2 * DEPTH, 3 * DEPTH)
        for core in range(2):
            dest = chip * 2 + core
            rows = slice(core * 8, core * 8 + 8)
            quart = slice(core * 8 + chip * 4, core * 8 + chip * 4 + 4)
            out_ref[dest, KV_ROWS : KV_ROWS + HALF, :] = query_ref[rows, 0, :, full].reshape(
                HALF, DEPTH
            )
            out_ref[dest, KV_ROWS + HALF : MSG_ROWS, :] = query_ref[
                quart, 0, :, DEPTH : 2 * DEPTH
            ].reshape(QUART, DEPTH)

    @pl.when(edited)
    def _():
        for core in range(2):
            rows = slice(core * 8, core * 8 + 8)
            for head in range(3):
                cols = slice(head * DEPTH, (head + 1) * DEPTH)
                place(
                    core,
                    head,
                    keys_ref[rows, 0, :, cols].reshape(HALF, DEPTH),
                    values_ref[rows, 0, :, cols].reshape(HALF, DEPTH),
                )

    @pl.when(jnp.logical_not(edited))
    def _():
        place_id = lax.broadcasted_iota(jnp.int32, (TOKS, TOKS), 0)
        source_id = lax.broadcasted_iota(jnp.int32, (TOKS, TOKS), 1)
        wanted = jnp.where(place_id < HALF, 2 * place_id, 2 * place_id - (TOKS - 1))
        sorter = (source_id == wanted).astype(jnp.float32).astype(jnp.bfloat16)
        for core in range(2):
            pairs = cache_ref[core * 8 : core * 8 + 8].reshape(TOKS, 3 * DEPTH)
            apart = jnp.dot(sorter, pairs, preferred_element_type=jnp.float32)
            apart = apart.astype(jnp.bfloat16)
            for head in range(3):
                cols = slice(head * DEPTH, (head + 1) * DEPTH)
                place(core, head, apart[0:HALF, cols], apart[HALF:TOKS, cols])


def pack(row_axes, listed_rows, cache, fresh):
    return pl.pallas_call(
        functools.partial(pack_kernel, row_axes),
        grid=(4,),
        in_specs=[
            smem(),
            pl.BlockSpec((16, 16, 2, 3 * DEPTH), lambda p: (0, 0, 0, p)),
            fresh_spec(0),
            fresh_spec(1),
            fresh_spec(2),
        ],
        out_specs=pl.BlockSpec((4, MSG_ROWS, DEPTH), lambda p: (p, 0, 0)),
        out_shape=jax.ShapeDtypeStruct((16, MSG_ROWS, DEPTH), jnp.bfloat16),
        cost_estimate=cost(0, 9 * 786432),
        compiler_params=pltpu.CompilerParams(vmem_limit_bytes=56 * MIB),
    )(listed_rows, cache, fresh, fresh, fresh)


def pick_kernel(rows_ref, got_ref, out_ref):
    bands = got_ref.shape[0]
    for slot in range(SLOTS):
        row = rows_ref[slot]
        rows = got_ref[jnp.minimum(row, bands - 1), KV_ROWS:MSG_ROWS, :]
        flag = jnp.where(row < bands, 1.0, 0.0)
        flags = jnp.full((SLOT_ROWS - Q_ROWS, DEPTH), flag, jnp.float32).astype(jnp.bfloat16)
        for dest in range(out_ref.shape[0]):
            out_ref[dest, slot, 0:Q_ROWS, :] = rows
            out_ref[dest, slot, Q_ROWS:SLOT_ROWS, :] = flags


def pick(listed_rows, received, copies):
    return pl.pallas_call(
        pick_kernel,
        in_specs=[smem(), vmem()],
        out_specs=vmem(),
        out_shape=jax.ShapeDtypeStruct((copies, SLOTS, SLOT_ROWS, DEPTH), jnp.bfloat16),
        cost_estimate=cost(0, 2 * 1703936),
        compiler_params=pltpu.CompilerParams(vmem_limit_bytes=16 * MIB),
    )(listed_rows, received)


def attend_rows(queries, kv_refs, head):
    fold = math.log2(math.e) / math.sqrt(DEPTH)
    row_max = total = acc = None
    tiles = KEY_BLOCK // HALF
    first = 2 * HALF * head
    for kv_ref in kv_refs:
        for block in range(kv_ref.shape[0] // tiles):
            rows = slice(block * tiles, (block + 1) * tiles)
            keys = kv_ref[rows, first : first + HALF, :].reshape(KEY_BLOCK, DEPTH)
            values = kv_ref[rows, first + HALF : first + 2 * HALF, :].reshape(KEY_BLOCK, DEPTH)
            scores = lax.dot_general(
                queries, keys, (((1,), (1,)), ((), ())), preferred_element_type=jnp.float32
            )
            scores = scores * fold
            block_max = jnp.max(scores, axis=1, keepdims=True)
            new_max = block_max if row_max is None else jnp.maximum(row_max, block_max)
            weights = jnp.exp2(scores - new_max)
            block_total = jnp.sum(weights, axis=1, keepdims=True)
            term = jnp.dot(
                weights.astype(jnp.bfloat16), values, preferred_element_type=jnp.float32
            )
            if row_max is None:
                total, acc = block_total, term
            else:
                shrink = jnp.exp2(row_max - new_max)
                total = total * shrink + block_total
                acc = acc * shrink + term
            row_max = new_max
    lse = jnp.broadcast_to(jnp.log2(total) + row_max, acc.shape)
    return (acc / total).astype(jnp.bfloat16), lse


def attend_kernel(valid_ref, q_ref, own_ref, other_ref, out_ref, table):
    slots = q_ref.shape[0]

    def note(slot, count):
        is_valid = valid_ref[slot]

        @pl.when(is_valid == 1)
        def _():
            table[count] = slot

        return count + is_valid

    count = lax.fori_loop(0, slots, note, jnp.int32(0))
    for extra in range(GROUP):
        table[count + extra] = table[0]

    kv_refs = (own_ref, other_ref)

    def body(group, carry):
        picks = [table[group * GROUP + i] for i in range(GROUP)]
        full = jnp.concatenate([q_ref[pick, 0:HALF, :] for pick in picks], axis=0)
        out_full, lse_full = attend_rows(full, kv_refs, 0)
        shared = jnp.concatenate([q_ref[pick, HALF:Q_ROWS, :] for pick in picks], axis=0)
        out_shared, lse_shared = attend_rows(shared, kv_refs, 1)
        row_ids = lax.broadcasted_iota(jnp.int32, (16, DEPTH), 0)
        for i, pick in enumerate(picks):
            out_ref[pick, 0:HALF, :] = out_full[i * HALF : (i + 1) * HALF]
            out_ref[pick, HALF:Q_ROWS, :] = out_shared[i * QUART : (i + 1) * QUART]
            lse_one = lse_shared[i * QUART : (i + 1) * QUART]
            pair = (
                jnp.transpose(lse_full[i * HALF : (i + 1) * HALF]),
                jnp.transpose(jnp.concatenate([lse_one, lse_one], axis=0)),
            )
            stats = jnp.zeros((16, DEPTH), jnp.float32)
            for j, lanes in enumerate(pair):
                rest = lanes[0:16]
                for term in range(3):
                    piece = rest.astype(jnp.bfloat16).astype(jnp.float32)
                    rest = rest - piece
                    stats = jnp.where(row_ids == 3 * j + term, piece, stats)
            out_ref[pick, Q_ROWS:SLOT_ROWS, :] = stats.astype(jnp.bfloat16)
        return carry

    lax.fori_loop(0, pl.cdiv(count, GROUP), body, 0)


def attend(valid, queries, own, other):
    slots = queries.shape[0]
    return pl.pallas_call(
        attend_kernel,
        in_specs=[smem(), vmem(), vmem(), vmem()],
        out_specs=vmem(),
        out_shape=jax.ShapeDtypeStruct((slots, SLOT_ROWS, DEPTH), jnp.bfloat16),
        scratch_shapes=[
            pltpu.SMEM((slots + GROUP,), jnp.int32),
        ],
        cost_estimate=cost(20 * 10**9, 8 * MIB),
        compiler_params=pltpu.CompilerParams(vmem_limit_bytes=48 * MIB),
    )(valid, queries, own, other)


def combine_kernel(rows_ref, part_ref, out_ref):
    out_ref[...] = jnp.zeros_like(out_ref)
    band_count = out_ref.shape[0]
    sources = part_ref.shape[0]
    for slot in range(SLOTS):
        row = rows_ref[slot]

        @pl.when(row < band_count)
        def _():
            stats = [
                part_ref[i, slot, Q_ROWS:SLOT_ROWS, :].astype(jnp.float32) for i in range(sources)
            ]
            for j, (first, size) in enumerate(((0, HALF), (HALF, QUART))):
                lses = [s[3 * j : 3 * j + 1] + s[3 * j + 1 : 3 * j + 2] + s[3 * j + 2 : 3 * j + 3] for s in stats]
                top = lses[0]
                for lse in lses[1:]:
                    top = jnp.maximum(top, lse)
                shares = [jnp.exp2(lse - top) for lse in lses]
                whole = shares[0]
                for share in shares[1:]:
                    whole = whole + share
                total = jnp.zeros((size, DEPTH), jnp.float32)
                for i in range(sources):
                    share = jnp.broadcast_to(shares[i] / whole, (DEPTH, DEPTH))
                    total = total + jnp.transpose(share)[0:size] * part_ref[
                        i, slot, first : first + size, :
                    ].astype(jnp.float32)
                out_ref[row, first : first + size, :] = total.astype(jnp.bfloat16)


def combine(listed_rows, partials, band_count):
    return pl.pallas_call(
        combine_kernel,
        in_specs=[smem(), vmem()],
        out_specs=vmem(),
        out_shape=jax.ShapeDtypeStruct((band_count, Q_ROWS, DEPTH), jnp.bfloat16),
        compiler_params=pltpu.CompilerParams(vmem_limit_bytes=24 * MIB),
    )(listed_rows, partials)


def unpack_kernel(in_ref, out_ref):
    for chip in range(in_ref.shape[0]):
        trio, second = chip // 2, chip % 2
        head = 3 * trio + 2 * second
        out_ref[:, head * DEPTH : (head + 1) * DEPTH] = in_ref[chip, 0, 0:HALF, :]
        shared = slice((3 * trio + 1) * DEPTH, (3 * trio + 2) * DEPTH)
        out_ref[second * QUART : (second + 1) * QUART, shared] = in_ref[chip, 0, HALF:Q_ROWS, :]


def unpack(received, features):
    chips = received.shape[0] // 2
    return pl.pallas_call(
        unpack_kernel,
        grid=(2,),
        in_specs=[pl.BlockSpec((chips, 1, Q_ROWS, DEPTH), lambda core: (0, core, 0, 0))],
        out_specs=pl.BlockSpec((HALF, features), lambda core: (core, 0)),
        out_shape=jax.ShapeDtypeStruct((TOKS, features), jnp.bfloat16),
        cost_estimate=cost(0, 2 * 786432),
    )(received.reshape(chips, 2, Q_ROWS, DEPTH))


def per_device(kv_cache, fresh_qkv, edit_list):
    tile_edge, tile_width, _, features = kv_cache.shape
    row_axes = ("chip", "core")
    band_count = lax.axis_size(row_axes)
    col_count = lax.axis_size("col")
    listed_rows = edit_list[:, 0]
    fresh = fresh_qkv.transpose(0, 2, 1, 3)
    message = pack(row_axes, listed_rows, kv_cache, fresh)
    own = lax.all_to_all(message, row_axes, 0, 0, tiled=True)
    other = lax.ppermute(own, "core", [(0, 1), (1, 0)])
    spread = pick(listed_rows, own, col_count)
    queries = lax.all_to_all(spread, "col", 0, 0, tiled=True)
    queries = queries.reshape(col_count * SLOTS, SLOT_ROWS, DEPTH)
    valid = queries[:, Q_ROWS, 0].astype(jnp.int32)

    partials = attend(valid, queries, own, other)
    partials = partials.reshape(col_count, SLOTS, SLOT_ROWS, DEPTH)
    partials = lax.all_to_all(partials, "col", 0, 0, tiled=True)
    finished = combine(listed_rows, partials, band_count)
    finished = lax.all_to_all(finished, row_axes, 0, 0, tiled=True)
    return unpack(finished, features).reshape(tile_edge, tile_width, features)


def solution(mesh):
    rows, cols = mesh.devices.shape
    fine = Mesh(mesh.devices.reshape(rows // 2, 2, cols), ("chip", "core", "col"))
    split = ("chip", "core")
    placed = (P(split, "col", None, None), P(split, "col", None, None), P(None, "col"))
    return jax.shard_map(
        per_device, mesh=fine, in_specs=placed, out_specs=P(split, "col", None), check_vma=False
    )
```

```python
import functools
import math

import jax
import jax.numpy as jnp
from jax import lax
from jax.experimental import pallas as pl
from jax.experimental.pallas import tpu as pltpu
from jax.sharding import Mesh, PartitionSpec as P

DEPTH = 128
SLOTS = 4
TOKS = 256
HALF = 128
QUART = 64
KV_ROWS = 4 * HALF
Q_ROWS = HALF + QUART
MSG_ROWS = KV_ROWS + Q_ROWS
SLOT_ROWS = Q_ROWS + 16
GROUP = 4
KEY_BLOCK = 512
MIB = 1024 * 1024


def vmem():
    return pl.BlockSpec(memory_space=pltpu.VMEM)


def smem():
    return pl.BlockSpec(memory_space=pltpu.SMEM)


def cost(flops, moved):
    return pl.CostEstimate(flops=flops, bytes_accessed=moved, transcendentals=0)


def fresh_spec(part):
    return pl.BlockSpec((16, 1, 16, 3 * DEPTH), lambda p: (0, part, 0, p))


def pack_kernel(row_axes, rows_ref, cache_ref, query_ref, keys_ref, values_ref, out_ref):
    my_row = lax.axis_index(row_axes)
    edited = rows_ref[0] == my_row
    for slot in range(1, SLOTS):
        edited = jnp.logical_or(edited, rows_ref[slot] == my_row)

    def place(core, head, keys, values):
        for chip in ((0,), (0, 1), (1,))[head]:
            first = 2 * HALF if head == 1 else 0
            out_ref[chip * 2 + core, first : first + HALF, :] = keys
            out_ref[chip * 2 + core, first + HALF : first + 2 * HALF, :] = values

    for chip in range(2):
        full = slice(0, DEPTH) if chip == 0 else slice(2 * DEPTH, 3 * DEPTH)
        for core in range(2):
            dest = chip * 2 + core
            rows = slice(core * 8, core * 8 + 8)
            quart = slice(core * 8 + chip * 4, core * 8 + chip * 4 + 4)
            out_ref[dest, KV_ROWS : KV_ROWS + HALF, :] = query_ref[rows, 0, :, full].reshape(
                HALF, DEPTH
            )
            out_ref[dest, KV_ROWS + HALF : MSG_ROWS, :] = query_ref[
                quart, 0, :, DEPTH : 2 * DEPTH
            ].reshape(QUART, DEPTH)

    @pl.when(edited)
    def _():
        for core in range(2):
            rows = slice(core * 8, core * 8 + 8)
            for head in range(3):
                cols = slice(head * DEPTH, (head + 1) * DEPTH)
                place(
                    core,
                    head,
                    keys_ref[rows, 0, :, cols].reshape(HALF, DEPTH),
                    values_ref[rows, 0, :, cols].reshape(HALF, DEPTH),
                )

    @pl.when(jnp.logical_not(edited))
    def _():
        place_id = lax.broadcasted_iota(jnp.int32, (TOKS, TOKS), 0)
        source_id = lax.broadcasted_iota(jnp.int32, (TOKS, TOKS), 1)
        wanted = jnp.where(place_id < HALF, 2 * place_id, 2 * place_id - (TOKS - 1))
        sorter = (source_id == wanted).astype(jnp.float32).astype(jnp.bfloat16)
        for core in range(2):
            pairs = cache_ref[core * 8 : core * 8 + 8].reshape(TOKS, 3 * DEPTH)
            apart = jnp.dot(sorter, pairs, preferred_element_type=jnp.float32)
            apart = apart.astype(jnp.bfloat16)
            for head in range(3):
                cols = slice(head * DEPTH, (head + 1) * DEPTH)
                place(core, head, apart[0:HALF, cols], apart[HALF:TOKS, cols])


def pack(row_axes, listed_rows, cache, fresh):
    return pl.pallas_call(
        functools.partial(pack_kernel, row_axes),
        grid=(4,),
        in_specs=[
            smem(),
            pl.BlockSpec((16, 16, 2, 3 * DEPTH), lambda p: (0, 0, 0, p)),
            fresh_spec(0),
            fresh_spec(1),
            fresh_spec(2),
        ],
        out_specs=pl.BlockSpec((4, MSG_ROWS, DEPTH), lambda p: (p, 0, 0)),
        out_shape=jax.ShapeDtypeStruct((16, MSG_ROWS, DEPTH), jnp.bfloat16),
        cost_estimate=cost(0, 9 * 786432),
        compiler_params=pltpu.CompilerParams(vmem_limit_bytes=56 * MIB),
    )(listed_rows, cache, fresh, fresh, fresh)


def pick_kernel(rows_ref, got_ref, out_ref):
    bands = got_ref.shape[0]
    for slot in range(SLOTS):
        row = rows_ref[slot]
        rows = got_ref[jnp.minimum(row, bands - 1), KV_ROWS:MSG_ROWS, :]
        flag = jnp.where(row < bands, 1.0, 0.0)
        flags = jnp.full((SLOT_ROWS - Q_ROWS, DEPTH), flag, jnp.float32).astype(jnp.bfloat16)
        for dest in range(out_ref.shape[0]):
            out_ref[dest, slot, 0:Q_ROWS, :] = rows
            out_ref[dest, slot, Q_ROWS:SLOT_ROWS, :] = flags


def pick(listed_rows, received, copies):
    return pl.pallas_call(
        pick_kernel,
        in_specs=[smem(), vmem()],
        out_specs=vmem(),
        out_shape=jax.ShapeDtypeStruct((copies, SLOTS, SLOT_ROWS, DEPTH), jnp.bfloat16),
        cost_estimate=cost(0, 2 * 1703936),
        compiler_params=pltpu.CompilerParams(vmem_limit_bytes=16 * MIB),
    )(listed_rows, received)


def widen_kernel(own_ref, other_ref, out_ref):
    for head in range(2):
        first = 2 * HALF * head + HALF
        for part, kv_ref in enumerate((own_ref, other_ref)):
            rows = slice(part * 2048, (part + 1) * 2048)
            out_ref[head, rows, 0:DEPTH] = kv_ref[:, first : first + HALF, :].reshape(2048, DEPTH)
        out_ref[head, :, DEPTH:] = jnp.ones((4096, DEPTH), jnp.bfloat16)


def widen(own, other):
    return pl.pallas_call(
        widen_kernel,
        in_specs=[vmem(), vmem()],
        out_specs=vmem(),
        out_shape=jax.ShapeDtypeStruct((2, 4096, 2 * DEPTH), jnp.bfloat16),
        cost_estimate=cost(0, 8 * MIB),
        compiler_params=pltpu.CompilerParams(vmem_limit_bytes=16 * MIB),
    )(own, other)


def attend_rows(queries, kv_refs, values_ref, head):
    fold = math.log2(math.e) / math.sqrt(DEPTH)
    row_max = acc = None
    tiles = KEY_BLOCK // HALF
    first = 2 * HALF * head
    for part, kv_ref in enumerate(kv_refs):
        for block in range(kv_ref.shape[0] // tiles):
            rows = slice(block * tiles, (block + 1) * tiles)
            keys = kv_ref[rows, first : first + HALF, :].reshape(KEY_BLOCK, DEPTH)
            scores = lax.dot_general(
                queries, keys, (((1,), (1,)), ((), ())), preferred_element_type=jnp.float32
            )
            scores = scores * fold
            block_max = jnp.max(scores, axis=1, keepdims=True)
            new_max = block_max if row_max is None else jnp.maximum(row_max, block_max)
            weights = jnp.exp2(scores - new_max).astype(jnp.bfloat16)
            start = part * 2048 + block * KEY_BLOCK
            term = jnp.dot(
                weights,
                values_ref[head, start : start + KEY_BLOCK, :],
                preferred_element_type=jnp.float32,
            )
            if row_max is None:
                acc = term
            else:
                acc = acc * jnp.exp2(row_max - new_max) + term
            row_max = new_max
    total = acc[:, DEPTH:]
    return (acc[:, :DEPTH] / total).astype(jnp.bfloat16), jnp.log2(total) + row_max


def attend_kernel(valid_ref, q_ref, own_ref, other_ref, values_ref, out_ref, table):
    slots = q_ref.shape[0]

    def note(slot, count):
        is_valid = valid_ref[slot]

        @pl.when(is_valid == 1)
        def _():
            table[count] = slot

        return count + is_valid

    count = lax.fori_loop(0, slots, note, jnp.int32(0))
    for extra in range(GROUP):
        table[count + extra] = table[0]

    kv_refs = (own_ref, other_ref)

    def attend_tiles(start, size):
        picks = [table[start + i] for i in range(size)]
        full = jnp.concatenate([q_ref[pick, 0:HALF, :] for pick in picks], axis=0)
        out_full, lse_full = attend_rows(full, kv_refs, values_ref, 0)
        shared = jnp.concatenate([q_ref[pick, HALF:Q_ROWS, :] for pick in picks], axis=0)
        out_shared, lse_shared = attend_rows(shared, kv_refs, values_ref, 1)
        row_ids = lax.broadcasted_iota(jnp.int32, (16, DEPTH), 0)
        for i, pick in enumerate(picks):
            out_ref[pick, 0:HALF, :] = out_full[i * HALF : (i + 1) * HALF]
            out_ref[pick, HALF:Q_ROWS, :] = out_shared[i * QUART : (i + 1) * QUART]
            lse_one = lse_shared[i * QUART : (i + 1) * QUART]
            pair = (
                jnp.transpose(lse_full[i * HALF : (i + 1) * HALF]),
                jnp.transpose(jnp.concatenate([lse_one, lse_one], axis=0)),
            )
            stats = jnp.zeros((16, DEPTH), jnp.float32)
            for j, lanes in enumerate(pair):
                rest = lanes[0:16]
                for term in range(3):
                    piece = rest.astype(jnp.bfloat16).astype(jnp.float32)
                    rest = rest - piece
                    stats = jnp.where(row_ids == 3 * j + term, piece, stats)
            out_ref[pick, Q_ROWS:SLOT_ROWS, :] = stats.astype(jnp.bfloat16)

    groups = (count + 1) // GROUP

    def body(group, carry):
        attend_tiles(group * GROUP, GROUP)
        return carry

    lax.fori_loop(0, groups, body, 0)

    @pl.when(groups * GROUP < count)
    def _():
        attend_tiles(groups * GROUP, 2)


def attend(valid, queries, own, other, values):
    slots = queries.shape[0]
    return pl.pallas_call(
        attend_kernel,
        in_specs=[smem(), vmem(), vmem(), vmem(), vmem()],
        out_specs=vmem(),
        out_shape=jax.ShapeDtypeStruct((slots, SLOT_ROWS, DEPTH), jnp.bfloat16),
        scratch_shapes=[pltpu.SMEM((slots + GROUP,), jnp.int32)],
        cost_estimate=cost(20 * 10**9, 8 * MIB),
        compiler_params=pltpu.CompilerParams(vmem_limit_bytes=40 * MIB),
    )(valid, queries, own, other, values)


def combine_kernel(rows_ref, part_ref, out_ref):
    out_ref[...] = jnp.zeros_like(out_ref)
    band_count = out_ref.shape[0]
    sources = part_ref.shape[0]
    for slot in range(SLOTS):
        row = rows_ref[slot]

        @pl.when(row < band_count)
        def _():
            stats = [
                part_ref[i, slot, Q_ROWS:SLOT_ROWS, :].astype(jnp.float32) for i in range(sources)
            ]
            for j, (first, size) in enumerate(((0, HALF), (HALF, QUART))):
                lses = [s[3 * j : 3 * j + 1] + s[3 * j + 1 : 3 * j + 2] + s[3 * j + 2 : 3 * j + 3] for s in stats]
                top = lses[0]
                for lse in lses[1:]:
                    top = jnp.maximum(top, lse)
                shares = [jnp.exp2(lse - top) for lse in lses]
                whole = shares[0]
                for share in shares[1:]:
                    whole = whole + share
                total = jnp.zeros((size, DEPTH), jnp.float32)
                for i in range(sources):
                    share = jnp.broadcast_to(shares[i] / whole, (DEPTH, DEPTH))
                    total = total + jnp.transpose(share)[0:size] * part_ref[
                        i, slot, first : first + size, :
                    ].astype(jnp.float32)
                out_ref[row, first : first + size, :] = total.astype(jnp.bfloat16)


def combine(listed_rows, partials, band_count):
    return pl.pallas_call(
        combine_kernel,
        in_specs=[smem(), vmem()],
        out_specs=vmem(),
        out_shape=jax.ShapeDtypeStruct((band_count, Q_ROWS, DEPTH), jnp.bfloat16),
        compiler_params=pltpu.CompilerParams(vmem_limit_bytes=24 * MIB),
    )(listed_rows, partials)


def unpack_kernel(in_ref, out_ref):
    for chip in range(in_ref.shape[0]):
        trio, second = chip // 2, chip % 2
        head = 3 * trio + 2 * second
        out_ref[:, head * DEPTH : (head + 1) * DEPTH] = in_ref[chip, 0, 0:HALF, :]
        shared = slice((3 * trio + 1) * DEPTH, (3 * trio + 2) * DEPTH)
        out_ref[second * QUART : (second + 1) * QUART, shared] = in_ref[chip, 0, HALF:Q_ROWS, :]


def unpack(received, features):
    chips = received.shape[0] // 2
    return pl.pallas_call(
        unpack_kernel,
        grid=(2,),
        in_specs=[pl.BlockSpec((chips, 1, Q_ROWS, DEPTH), lambda core: (0, core, 0, 0))],
        out_specs=pl.BlockSpec((HALF, features), lambda core: (core, 0)),
        out_shape=jax.ShapeDtypeStruct((TOKS, features), jnp.bfloat16),
        cost_estimate=cost(0, 2 * 786432),
    )(received.reshape(chips, 2, Q_ROWS, DEPTH))


def per_device(kv_cache, fresh_qkv, edit_list):
    tile_edge, tile_width, _, features = kv_cache.shape
    row_axes = ("chip", "core")
    band_count = lax.axis_size(row_axes)
    col_count = lax.axis_size("col")
    listed_rows = edit_list[:, 0]
    fresh = fresh_qkv.transpose(0, 2, 1, 3)
    message = pack(row_axes, listed_rows, kv_cache, fresh)
    own = lax.all_to_all(message, row_axes, 0, 0, tiled=True)
    other = lax.ppermute(own, "core", [(0, 1), (1, 0)])
    spread = pick(listed_rows, own, col_count)
    queries = lax.all_to_all(spread, "col", 0, 0, tiled=True)
    queries = queries.reshape(col_count * SLOTS, SLOT_ROWS, DEPTH)
    valid = queries[:, Q_ROWS, 0].astype(jnp.int32)

    partials = attend(valid, queries, own, other, widen(own, other))
    partials = partials.reshape(col_count, SLOTS, SLOT_ROWS, DEPTH)
    partials = lax.all_to_all(partials, "col", 0, 0, tiled=True)
    finished = combine(listed_rows, partials, band_count)
    finished = lax.all_to_all(finished, row_axes, 0, 0, tiled=True)
    return unpack(finished, features).reshape(tile_edge, tile_width, features)


def solution(mesh):
    rows, cols = mesh.devices.shape
    fine = Mesh(mesh.devices.reshape(rows // 2, 2, cols), ("chip", "core", "col"))
    split = ("chip", "core")
    placed = (P(split, "col", None, None), P(split, "col", None, None), P(None, "col"))
    return jax.shard_map(
        per_device, mesh=fine, in_specs=placed, out_specs=P(split, "col", None), check_vma=False
    )
```

```python
import math

import jax
import jax.numpy as jnp
from jax import lax
from jax.experimental import pallas as pl
from jax.experimental.pallas import tpu as pltpu
from jax.sharding import Mesh, PartitionSpec as P

DEPTH = 128
SLOTS = 4
TOKS = 256
HALF = 128
QUART = 64
KV_ROWS = 4 * TOKS
Q_ROWS = HALF + QUART
SLOT_ROWS = Q_ROWS + 16
GROUP = 4
KEY_BLOCK = 512
MIB = 1024 * 1024


def vmem():
    return pl.BlockSpec(memory_space=pltpu.VMEM)


def smem():
    return pl.BlockSpec(memory_space=pltpu.SMEM)


CHIP = ("y", "z_lo")
ROW = CHIP + ("core",)


STEPS = (5, 4, 7, 2, 3, 6, 1)


def flip():
    return lax.axis_index("col") // (lax.axis_size("col") // 2)


def across(x):
    cols = lax.axis_size("col")
    near, far = list(range(cols // 2)), list(range(cols // 2, cols))
    groups = [near + [cols + i for i in far], [cols + i for i in near] + far]
    return lax.all_to_all(x, ("z_lo", "col"), 0, 0, axis_index_groups=groups, tiled=True)


def cost(flops, moved):
    return pl.CostEstimate(flops=flops, bytes_accessed=moved, transcendentals=0)


def pack_query_kernel(in_ref, out_ref):
    for chip in range(out_ref.shape[0]):
        trio, second = chip // 2, chip % 2
        head = 3 * trio + 2 * second
        dest = jnp.bitwise_xor(chip, flip())
        out_ref[dest, 0, 0:HALF, :] = in_ref[:, 0, :, head * DEPTH : (head + 1) * DEPTH].reshape(
            HALF, DEPTH
        )
        shared = slice((3 * trio + 1) * DEPTH, (3 * trio + 2) * DEPTH)
        rows = slice(second * 4, second * 4 + 4)
        out_ref[dest, 0, HALF:Q_ROWS, :] = in_ref[rows, 0, :, shared].reshape(QUART, DEPTH)


def pack_query(fresh, chips):
    features = fresh.shape[3]
    out = pl.pallas_call(
        pack_query_kernel,
        grid=(2,),
        in_specs=[pl.BlockSpec((8, 1, 16, features), lambda core: (core, 0, 0, 0))],
        out_specs=pl.BlockSpec((chips, 1, Q_ROWS, DEPTH), lambda core: (0, core, 0, 0)),
        out_shape=jax.ShapeDtypeStruct((chips, 2, Q_ROWS, DEPTH), jnp.bfloat16),
        cost_estimate=cost(0, 2 * 786432),
    )(fresh)
    return out.reshape(2 * chips, Q_ROWS, DEPTH)


def fresh_spec(part):
    return pl.BlockSpec((16, 1, 16, 3 * DEPTH), lambda p: (0, part, 0, p))


def pack_kernel(rows_ref, cache_ref, keys_ref, values_ref, *refs):
    out_refs, sorted_ref = refs[:-1], refs[-1]
    my_chip = lax.axis_index(CHIP)
    my_row = 2 * my_chip + lax.axis_index("core")
    my_chip = jnp.bitwise_xor(my_chip, flip())
    edited = rows_ref[0] == my_row
    for slot in range(1, SLOTS):
        edited = jnp.logical_or(edited, rows_ref[slot] == my_row)

    @pl.when(edited)
    def _():
        for part, ref in enumerate((keys_ref, values_ref)):
            sorted_ref[part] = ref[...].reshape(TOKS, 3 * DEPTH)

    @pl.when(jnp.logical_not(edited))
    def _():
        place_id = lax.broadcasted_iota(jnp.int32, (TOKS, TOKS), 0)
        source_id = lax.broadcasted_iota(jnp.int32, (TOKS, TOKS), 1)
        wanted = jnp.where(place_id < HALF, 2 * place_id, 2 * place_id - (TOKS - 1))
        sorter = (source_id == wanted).astype(jnp.float32).astype(jnp.bfloat16)
        for half in range(2):
            pairs = cache_ref[half * 8 : half * 8 + 8].reshape(TOKS, 3 * DEPTH)
            apart = jnp.dot(sorter, pairs, preferred_element_type=jnp.float32)
            apart = apart.astype(jnp.bfloat16)
            for part in range(2):
                sorted_ref[part, half * HALF : (half + 1) * HALF, :] = apart[
                    part * HALF : (part + 1) * HALF
                ]

    pair = jnp.bitwise_xor(pl.program_id(0), my_chip // 2)
    swapped = jnp.bitwise_and(my_chip, 1)
    for j in range(len(out_refs) // 2):
        for i in range(2):
            second = jnp.bitwise_xor(swapped, i)

            for which in range(2):

                @pl.when(jnp.logical_and(pair == j, second == which))
                def _():
                    full = slice(2 * which * DEPTH, (2 * which + 1) * DEPTH)
                    out_ref = out_refs[((0,) + STEPS).index(2 * j + i)]
                    for part in range(2):
                        out_ref[part * TOKS : (part + 1) * TOKS, :] = sorted_ref[part, :, full]
                        out_ref[(2 + part) * TOKS : (3 + part) * TOKS, :] = sorted_ref[
                            part, :, DEPTH : 2 * DEPTH
                        ]


def pack(listed_rows, cache, fresh, chips):
    return pl.pallas_call(
        pack_kernel,
        grid=(chips // 2,),
        in_specs=[
            smem(),
            pl.BlockSpec((16, 16, 2, 3 * DEPTH), lambda p: (0, 0, 0, p)),
            fresh_spec(1),
            fresh_spec(2),
        ],
        out_specs=[vmem()] * chips,
        out_shape=[jax.ShapeDtypeStruct((KV_ROWS, DEPTH), jnp.bfloat16)] * chips,
        scratch_shapes=[pltpu.VMEM((2, TOKS, 3 * DEPTH), jnp.bfloat16)],
        cost_estimate=cost(0, 7 * 786432),
        compiler_params=pltpu.CompilerParams(vmem_limit_bytes=20 * MIB),
    )(listed_rows, cache, fresh, fresh)


def join_kernel(*refs):
    count = len(refs) - 2
    out_ref, arrived = refs[count], refs[count + 1]
    copies = [pltpu.make_async_copy(refs[i], out_ref.at[i], arrived.at[i]) for i in range(count)]
    for copy in copies:
        copy.start()
    for copy in copies:
        copy.wait()


def join(pieces):
    return pl.pallas_call(
        join_kernel,
        in_specs=[pl.BlockSpec(memory_space=pl.ANY)] * len(pieces),
        out_specs=vmem(),
        out_shape=jax.ShapeDtypeStruct((len(pieces), KV_ROWS, DEPTH), jnp.bfloat16),
        scratch_shapes=[pltpu.SemaphoreType.DMA((len(pieces),))],
        cost_estimate=cost(0, 4 * MIB),
        compiler_params=pltpu.CompilerParams(vmem_limit_bytes=16 * MIB),
    )(*pieces)


def pick_kernel(rows_ref, got_ref, out_ref):
    bands = got_ref.shape[0]
    for slot in range(SLOTS):
        row = rows_ref[slot]
        rows = got_ref[jnp.minimum(row, bands - 1)]
        flag = jnp.where(row < bands, 1.0, 0.0)
        flags = jnp.full((SLOT_ROWS - Q_ROWS, DEPTH), flag, jnp.float32).astype(jnp.bfloat16)
        for dest in range(out_ref.shape[0]):
            out_ref[dest, slot, 0:Q_ROWS, :] = rows
            out_ref[dest, slot, Q_ROWS:SLOT_ROWS, :] = flags


def pick(listed_rows, received, copies):
    return pl.pallas_call(
        pick_kernel,
        in_specs=[smem(), vmem()],
        out_specs=vmem(),
        out_shape=jax.ShapeDtypeStruct((copies, SLOTS, SLOT_ROWS, DEPTH), jnp.bfloat16),
        cost_estimate=cost(0, 2 * 1703936),
        compiler_params=pltpu.CompilerParams(vmem_limit_bytes=16 * MIB),
    )(listed_rows, received)


def widen_kernel(own_ref, other_ref, out_ref):
    for head in range(2):
        first = 2 * TOKS * head + TOKS
        for part, kv_ref in enumerate((own_ref, other_ref)):
            rows = slice(part * 2048, (part + 1) * 2048)
            out_ref[head, rows, 0:DEPTH] = kv_ref[:, first : first + TOKS, :].reshape(2048, DEPTH)
        out_ref[head, :, DEPTH:] = jnp.ones((4096, DEPTH), jnp.bfloat16)


def widen(own, other):
    return pl.pallas_call(
        widen_kernel,
        in_specs=[vmem(), vmem()],
        out_specs=vmem(),
        out_shape=jax.ShapeDtypeStruct((2, 4096, 2 * DEPTH), jnp.bfloat16),
        cost_estimate=cost(0, 8 * MIB),
        compiler_params=pltpu.CompilerParams(vmem_limit_bytes=16 * MIB),
    )(own, other)


def attend_rows(queries, kv_refs, values_ref, head):
    fold = math.log2(math.e) / math.sqrt(DEPTH)
    row_max = acc = None
    tiles = KEY_BLOCK // TOKS
    first = 2 * TOKS * head
    for part, kv_ref in enumerate(kv_refs):
        for block in range(kv_ref.shape[0] // tiles):
            rows = slice(block * tiles, (block + 1) * tiles)
            keys = kv_ref[rows, first : first + TOKS, :].reshape(KEY_BLOCK, DEPTH)
            scores = lax.dot_general(
                queries, keys, (((1,), (1,)), ((), ())), preferred_element_type=jnp.float32
            )
            scores = scores * fold
            block_max = jnp.max(scores, axis=1, keepdims=True)
            new_max = block_max if row_max is None else jnp.maximum(row_max, block_max)
            weights = jnp.exp2(scores - new_max).astype(jnp.bfloat16)
            start = part * 2048 + block * KEY_BLOCK
            term = jnp.dot(
                weights,
                values_ref[head, start : start + KEY_BLOCK, :],
                preferred_element_type=jnp.float32,
            )
            if row_max is None:
                acc = term
            else:
                acc = acc * jnp.exp2(row_max - new_max) + term
            row_max = new_max
    total = acc[:, DEPTH:]
    return (acc[:, :DEPTH] / total).astype(jnp.bfloat16), jnp.log2(total) + row_max


def attend_kernel(valid_ref, q_ref, own_ref, other_ref, values_ref, out_ref, table):
    slots = q_ref.shape[0]

    def note(slot, count):
        is_valid = valid_ref[slot]

        @pl.when(is_valid == 1)
        def _():
            table[count] = slot

        return count + is_valid

    count = lax.fori_loop(0, slots, note, jnp.int32(0))
    for extra in range(GROUP):
        table[count + extra] = table[0]

    kv_refs = (own_ref, other_ref)

    def attend_tiles(start, size):
        picks = [table[start + i] for i in range(size)]
        full = jnp.concatenate([q_ref[pick, 0:HALF, :] for pick in picks], axis=0)
        out_full, lse_full = attend_rows(full, kv_refs, values_ref, 0)
        shared = jnp.concatenate([q_ref[pick, HALF:Q_ROWS, :] for pick in picks], axis=0)
        out_shared, lse_shared = attend_rows(shared, kv_refs, values_ref, 1)
        row_ids = lax.broadcasted_iota(jnp.int32, (16, DEPTH), 0)
        for i, pick in enumerate(picks):
            out_ref[pick, 0:HALF, :] = out_full[i * HALF : (i + 1) * HALF]
            out_ref[pick, HALF:Q_ROWS, :] = out_shared[i * QUART : (i + 1) * QUART]
            lse_one = lse_shared[i * QUART : (i + 1) * QUART]
            pair = (
                jnp.transpose(lse_full[i * HALF : (i + 1) * HALF]),
                jnp.transpose(jnp.concatenate([lse_one, lse_one], axis=0)),
            )
            stats = jnp.zeros((16, DEPTH), jnp.float32)
            for j, lanes in enumerate(pair):
                rest = lanes[0:16]
                for term in range(3):
                    piece = rest.astype(jnp.bfloat16).astype(jnp.float32)
                    rest = rest - piece
                    stats = jnp.where(row_ids == 3 * j + term, piece, stats)
            out_ref[pick, Q_ROWS:SLOT_ROWS, :] = stats.astype(jnp.bfloat16)

    groups = (count + 1) // GROUP

    def body(group, carry):
        attend_tiles(group * GROUP, GROUP)
        return carry

    lax.fori_loop(0, groups, body, 0)

    @pl.when(groups * GROUP < count)
    def _():
        attend_tiles(groups * GROUP, 2)


def attend(valid, queries, own, other, values):
    slots = queries.shape[0]
    return pl.pallas_call(
        attend_kernel,
        in_specs=[smem(), vmem(), vmem(), vmem(), vmem()],
        out_specs=vmem(),
        out_shape=jax.ShapeDtypeStruct((slots, SLOT_ROWS, DEPTH), jnp.bfloat16),
        scratch_shapes=[pltpu.SMEM((slots + GROUP,), jnp.int32)],
        cost_estimate=cost(20 * 10**9, 8 * MIB),
        compiler_params=pltpu.CompilerParams(vmem_limit_bytes=30 * MIB),
    )(valid, queries, own, other, values)


def combine_kernel(rows_ref, part_ref, out_ref):
    out_ref[...] = jnp.zeros_like(out_ref)
    band_count = out_ref.shape[0]
    sources = part_ref.shape[0]
    for slot in range(SLOTS):
        row = rows_ref[slot]

        @pl.when(row < band_count)
        def _():
            stats = [
                part_ref[i, slot, Q_ROWS:SLOT_ROWS, :].astype(jnp.float32) for i in range(sources)
            ]
            for j, (first, size) in enumerate(((0, HALF), (HALF, QUART))):
                lses = [s[3 * j : 3 * j + 1] + s[3 * j + 1 : 3 * j + 2] + s[3 * j + 2 : 3 * j + 3] for s in stats]
                top = lses[0]
                for lse in lses[1:]:
                    top = jnp.maximum(top, lse)
                shares = [jnp.exp2(lse - top) for lse in lses]
                whole = shares[0]
                for share in shares[1:]:
                    whole = whole + share
                total = jnp.zeros((size, DEPTH), jnp.float32)
                for i in range(sources):
                    share = jnp.broadcast_to(shares[i] / whole, (DEPTH, DEPTH))
                    total = total + jnp.transpose(share)[0:size] * part_ref[
                        i, slot, first : first + size, :
                    ].astype(jnp.float32)
                out_ref[row, first : first + size, :] = total.astype(jnp.bfloat16)


def combine(listed_rows, partials, band_count):
    return pl.pallas_call(
        combine_kernel,
        in_specs=[smem(), vmem()],
        out_specs=vmem(),
        out_shape=jax.ShapeDtypeStruct((band_count, Q_ROWS, DEPTH), jnp.bfloat16),
        compiler_params=pltpu.CompilerParams(vmem_limit_bytes=24 * MIB),
    )(listed_rows, partials)


def unpack_kernel(in_ref, out_ref):
    for chip in range(in_ref.shape[0]):
        trio, second = chip // 2, chip % 2
        head = 3 * trio + 2 * second
        source = jnp.bitwise_xor(chip, flip())
        out_ref[:, head * DEPTH : (head + 1) * DEPTH] = in_ref[source, 0, 0:HALF, :]
        shared = slice((3 * trio + 1) * DEPTH, (3 * trio + 2) * DEPTH)
        out_ref[second * QUART : (second + 1) * QUART, shared] = in_ref[source, 0, HALF:Q_ROWS, :]


def unpack(received, features):
    chips = received.shape[0] // 2
    return pl.pallas_call(
        unpack_kernel,
        grid=(2,),
        in_specs=[pl.BlockSpec((chips, 1, Q_ROWS, DEPTH), lambda core: (0, core, 0, 0))],
        out_specs=pl.BlockSpec((HALF, features), lambda core: (core, 0)),
        out_shape=jax.ShapeDtypeStruct((TOKS, features), jnp.bfloat16),
        cost_estimate=cost(0, 2 * 786432),
    )(received.reshape(chips, 2, Q_ROWS, DEPTH))


def per_device(kv_cache, fresh_qkv, edit_list):
    tile_edge, tile_width, _, features = kv_cache.shape
    band_count = lax.axis_size(ROW)
    col_count = lax.axis_size("col")
    listed_rows = edit_list[:, 0]
    fresh = fresh_qkv.transpose(0, 2, 1, 3)
    chips = lax.axis_size(CHIP)
    query_message = pack_query(fresh, chips)
    got_query = lax.all_to_all(query_message, ROW, 0, 0, tiled=True)
    fresh, query_message = lax.optimization_barrier((fresh, query_message))
    messages = pack(listed_rows, kv_cache, fresh, chips)
    spread = pick(listed_rows, got_query, col_count)
    messages, spread = lax.optimization_barrier((messages, spread))
    pieces = [messages[0]]
    for step, message in zip(STEPS, messages[1:]):
        pairs = [(i, i ^ step) for i in range(chips)]
        pieces.append(lax.ppermute(message, CHIP, pairs))
    queries = across(spread)
    pieces, queries = lax.optimization_barrier((pieces, queries))
    own = join(pieces)
    other = lax.ppermute(own, "core", [(0, 1), (1, 0)])
    queries = queries.reshape(col_count * SLOTS, SLOT_ROWS, DEPTH)
    valid = queries[:, Q_ROWS, 0].astype(jnp.int32)

    partials = attend(valid, queries, own, other, widen(own, other))
    partials = partials.reshape(col_count, SLOTS, SLOT_ROWS, DEPTH)
    partials = across(partials)
    finished = combine(listed_rows, partials, band_count)
    finished = lax.all_to_all(finished, ROW, 0, 0, tiled=True)
    return unpack(finished, features).reshape(tile_edge, tile_width, features)


def solution(mesh):
    rows, cols = mesh.devices.shape
    fine = Mesh(mesh.devices.reshape(rows // 4, 2, 2, cols), ROW + ("col",))
    placed = (P(ROW, "col", None, None), P(ROW, "col", None, None), P(None, "col"))
    return jax.shard_map(
        per_device, mesh=fine, in_specs=placed, out_specs=P(ROW, "col", None), check_vma=False
    )
```

```python
import math

import jax
import jax.numpy as jnp
from jax import lax
from jax.experimental import pallas as pl
from jax.experimental.pallas import tpu as pltpu
from jax.sharding import Mesh, PartitionSpec as P

DEPTH = 128
SLOTS = 4
TOKS = 256
HALF = 128
QUART = 64
KV_ROWS = 4 * HALF
Q_ROWS = HALF + QUART
SLOT_ROWS = Q_ROWS + 16
GROUP = 4
KEY_BLOCK = 512
MIB = 1024 * 1024


def vmem():
    return pl.BlockSpec(memory_space=pltpu.VMEM)


def smem():
    return pl.BlockSpec(memory_space=pltpu.SMEM)


CHIP = ("y", "z_lo")
ROW = CHIP + ("core",)


def flip():
    return lax.axis_index("col") // (lax.axis_size("col") // 2)


def shift(x, step):
    cols = lax.axis_size("col")
    far = step // (cols // 2)
    pairs = [(i, i ^ (far * cols + step)) for i in range(2 * cols)]
    return lax.ppermute(x, ("z_lo", "col"), pairs)


def across(x):
    cols = lax.axis_size("col")
    near, far = list(range(cols // 2)), list(range(cols // 2, cols))
    groups = [near + [cols + i for i in far], [cols + i for i in near] + far]
    return lax.all_to_all(x, ("z_lo", "col"), 0, 0, axis_index_groups=groups, tiled=True)


def cost(flops, moved):
    return pl.CostEstimate(flops=flops, bytes_accessed=moved, transcendentals=0)


def pack_query_kernel(in_ref, out_ref):
    for chip in range(out_ref.shape[0]):
        trio, second = chip // 2, chip % 2
        head = 3 * trio + 2 * second
        dest = jnp.bitwise_xor(chip, flip())
        out_ref[dest, 0, 0:HALF, :] = in_ref[:, 0, :, head * DEPTH : (head + 1) * DEPTH].reshape(
            HALF, DEPTH
        )
        shared = slice((3 * trio + 1) * DEPTH, (3 * trio + 2) * DEPTH)
        rows = slice(second * 4, second * 4 + 4)
        out_ref[dest, 0, HALF:Q_ROWS, :] = in_ref[rows, 0, :, shared].reshape(QUART, DEPTH)


def pack_query(fresh, chips):
    features = fresh.shape[3]
    out = pl.pallas_call(
        pack_query_kernel,
        grid=(2,),
        in_specs=[pl.BlockSpec((8, 1, 16, features), lambda core: (core, 0, 0, 0))],
        out_specs=pl.BlockSpec((chips, 1, Q_ROWS, DEPTH), lambda core: (0, core, 0, 0)),
        out_shape=jax.ShapeDtypeStruct((chips, 2, Q_ROWS, DEPTH), jnp.bfloat16),
        cost_estimate=cost(0, 2 * 786432),
    )(fresh)
    return out.reshape(2 * chips, Q_ROWS, DEPTH)


def fresh_spec(part):
    return pl.BlockSpec((16, 1, 16, 3 * DEPTH), lambda p: (0, part, 0, p))


def pack_kernel(rows_ref, cache_ref, keys_ref, values_ref, out_ref, sorted_ref):
    my_row = lax.axis_index(ROW)
    edited = rows_ref[0] == my_row
    for slot in range(1, SLOTS):
        edited = jnp.logical_or(edited, rows_ref[slot] == my_row)

    @pl.when(edited)
    def _():
        for part, ref in enumerate((keys_ref, values_ref)):
            sorted_ref[part] = ref[...].reshape(TOKS, 3 * DEPTH)

    @pl.when(jnp.logical_not(edited))
    def _():
        place_id = lax.broadcasted_iota(jnp.int32, (TOKS, TOKS), 0)
        source_id = lax.broadcasted_iota(jnp.int32, (TOKS, TOKS), 1)
        wanted = jnp.where(place_id < HALF, 2 * place_id, 2 * place_id - (TOKS - 1))
        sorter = (source_id == wanted).astype(jnp.float32).astype(jnp.bfloat16)
        for half in range(2):
            pairs = cache_ref[half * 8 : half * 8 + 8].reshape(TOKS, 3 * DEPTH)
            apart = jnp.dot(sorter, pairs, preferred_element_type=jnp.float32)
            apart = apart.astype(jnp.bfloat16)
            for part in range(2):
                sorted_ref[part, half * HALF : (half + 1) * HALF, :] = apart[
                    part * HALF : (part + 1) * HALF
                ]

    for chip in range(2):
        dest = jnp.bitwise_xor(chip, flip())
        for core in range(2):
            toks = slice(core * HALF, (core + 1) * HALF)
            for i, head in enumerate((2 * chip, 1)):
                cols = slice(head * DEPTH, (head + 1) * DEPTH)
                for part in range(2):
                    first = (2 * i + part) * HALF
                    out_ref[2 * dest + core, first : first + HALF, :] = sorted_ref[part, toks, cols]


def pack(listed_rows, cache, fresh):
    return pl.pallas_call(
        pack_kernel,
        grid=(4,),
        in_specs=[
            smem(),
            pl.BlockSpec((16, 16, 2, 3 * DEPTH), lambda p: (0, 0, 0, p)),
            fresh_spec(1),
            fresh_spec(2),
        ],
        out_specs=pl.BlockSpec((4, KV_ROWS, DEPTH), lambda p: (p, 0, 0)),
        out_shape=jax.ShapeDtypeStruct((16, KV_ROWS, DEPTH), jnp.bfloat16),
        scratch_shapes=[pltpu.VMEM((2, TOKS, 3 * DEPTH), jnp.bfloat16)],
        cost_estimate=cost(0, 7 * 786432),
        compiler_params=pltpu.CompilerParams(vmem_limit_bytes=20 * MIB),
    )(listed_rows, cache, fresh, fresh)


def join_kernel(*refs):
    count = len(refs) - 2
    out_ref, arrived = refs[count], refs[count + 1]
    copies = [pltpu.make_async_copy(refs[i], out_ref.at[i], arrived.at[i]) for i in range(count)]
    for copy in copies:
        copy.start()
    for copy in copies:
        copy.wait()


def join(pieces):
    return pl.pallas_call(
        join_kernel,
        in_specs=[pl.BlockSpec(memory_space=pl.ANY)] * len(pieces),
        out_specs=vmem(),
        out_shape=jax.ShapeDtypeStruct((len(pieces),) + pieces[0].shape, jnp.bfloat16),
        scratch_shapes=[pltpu.SemaphoreType.DMA((len(pieces),))],
        cost_estimate=cost(0, 4 * MIB),
        compiler_params=pltpu.CompilerParams(vmem_limit_bytes=16 * MIB),
    )(*pieces)


def pick_kernel(rows_ref, got_ref, out_ref):
    bands = got_ref.shape[0]
    for slot in range(SLOTS):
        row = rows_ref[slot]
        rows = got_ref[jnp.minimum(row, bands - 1)]
        flag = jnp.where(row < bands, 1.0, 0.0)
        flags = jnp.full((SLOT_ROWS - Q_ROWS, DEPTH), flag, jnp.float32).astype(jnp.bfloat16)
        out_ref[slot, 0:Q_ROWS, :] = rows
        out_ref[slot, Q_ROWS:SLOT_ROWS, :] = flags


def pick(listed_rows, received):
    return pl.pallas_call(
        pick_kernel,
        in_specs=[smem(), vmem()],
        out_specs=vmem(),
        out_shape=jax.ShapeDtypeStruct((SLOTS, SLOT_ROWS, DEPTH), jnp.bfloat16),
        cost_estimate=cost(0, 2 * 212992),
        compiler_params=pltpu.CompilerParams(vmem_limit_bytes=16 * MIB),
    )(listed_rows, received)


def widen_kernel(own_ref, other_ref, out_ref):
    for head in range(2):
        first = 2 * HALF * head + HALF
        for part, kv_ref in enumerate((own_ref, other_ref)):
            rows = slice(part * 2048, (part + 1) * 2048)
            out_ref[head, rows, 0:DEPTH] = kv_ref[:, first : first + HALF, :].reshape(2048, DEPTH)
        out_ref[head, :, DEPTH:] = jnp.ones((4096, DEPTH), jnp.bfloat16)


def widen(own, other):
    return pl.pallas_call(
        widen_kernel,
        in_specs=[vmem(), vmem()],
        out_specs=vmem(),
        out_shape=jax.ShapeDtypeStruct((2, 4096, 2 * DEPTH), jnp.bfloat16),
        cost_estimate=cost(0, 8 * MIB),
        compiler_params=pltpu.CompilerParams(vmem_limit_bytes=16 * MIB),
    )(own, other)


def attend_rows(queries, kv_refs, values_ref, head):
    fold = math.log2(math.e) / math.sqrt(DEPTH)
    row_max = acc = None
    tiles = KEY_BLOCK // HALF
    first = 2 * HALF * head
    for part, kv_ref in enumerate(kv_refs):
        for block in range(kv_ref.shape[0] // tiles):
            rows = slice(block * tiles, (block + 1) * tiles)
            keys = kv_ref[rows, first : first + HALF, :].reshape(KEY_BLOCK, DEPTH)
            scores = lax.dot_general(
                queries, keys, (((1,), (1,)), ((), ())), preferred_element_type=jnp.float32
            )
            scores = scores * fold
            block_max = jnp.max(scores, axis=1, keepdims=True)
            new_max = block_max if row_max is None else jnp.maximum(row_max, block_max)
            weights = jnp.exp2(scores - new_max).astype(jnp.bfloat16)
            start = part * 2048 + block * KEY_BLOCK
            term = jnp.dot(
                weights,
                values_ref[head, start : start + KEY_BLOCK, :],
                preferred_element_type=jnp.float32,
            )
            if row_max is None:
                acc = term
            else:
                acc = acc * jnp.exp2(row_max - new_max) + term
            row_max = new_max
    total = acc[:, DEPTH:]
    return (acc[:, :DEPTH] / total).astype(jnp.bfloat16), jnp.log2(total) + row_max


def attend_kernel(valid_ref, q_ref, own_ref, other_ref, values_ref, out_ref, table):
    slots = q_ref.shape[0]

    def note(slot, count):
        is_valid = valid_ref[slot]

        @pl.when(is_valid == 1)
        def _():
            table[count] = slot

        return count + is_valid

    count = lax.fori_loop(0, slots, note, jnp.int32(0))
    for extra in range(GROUP):
        table[count + extra] = table[0]

    kv_refs = (own_ref, other_ref)

    def attend_tiles(start, size):
        picks = [table[start + i] for i in range(size)]
        full = jnp.concatenate([q_ref[pick, 0:HALF, :] for pick in picks], axis=0)
        out_full, lse_full = attend_rows(full, kv_refs, values_ref, 0)
        shared = jnp.concatenate([q_ref[pick, HALF:Q_ROWS, :] for pick in picks], axis=0)
        out_shared, lse_shared = attend_rows(shared, kv_refs, values_ref, 1)
        row_ids = lax.broadcasted_iota(jnp.int32, (16, DEPTH), 0)
        picks = [jnp.bitwise_xor(pick, SLOTS * lax.axis_index("col")) for pick in picks]
        for i, pick in enumerate(picks):
            out_ref[pick, 0:HALF, :] = out_full[i * HALF : (i + 1) * HALF]
            out_ref[pick, HALF:Q_ROWS, :] = out_shared[i * QUART : (i + 1) * QUART]
            lse_one = lse_shared[i * QUART : (i + 1) * QUART]
            pair = (
                jnp.transpose(lse_full[i * HALF : (i + 1) * HALF]),
                jnp.transpose(jnp.concatenate([lse_one, lse_one], axis=0)),
            )
            stats = jnp.zeros((16, DEPTH), jnp.float32)
            for j, lanes in enumerate(pair):
                rest = lanes[0:16]
                for term in range(3):
                    piece = rest.astype(jnp.bfloat16).astype(jnp.float32)
                    rest = rest - piece
                    stats = jnp.where(row_ids == 3 * j + term, piece, stats)
            out_ref[pick, Q_ROWS:SLOT_ROWS, :] = stats.astype(jnp.bfloat16)

    groups = (count + 1) // GROUP

    def body(group, carry):
        attend_tiles(group * GROUP, GROUP)
        return carry

    lax.fori_loop(0, groups, body, 0)

    @pl.when(groups * GROUP < count)
    def _():
        attend_tiles(groups * GROUP, 2)


def attend(valid, queries, own, other, values):
    slots = queries.shape[0]
    return pl.pallas_call(
        attend_kernel,
        in_specs=[smem(), vmem(), vmem(), vmem(), vmem()],
        out_specs=vmem(),
        out_shape=jax.ShapeDtypeStruct((slots, SLOT_ROWS, DEPTH), jnp.bfloat16),
        scratch_shapes=[pltpu.SMEM((slots + GROUP,), jnp.int32)],
        cost_estimate=cost(20 * 10**9, 8 * MIB),
        compiler_params=pltpu.CompilerParams(vmem_limit_bytes=30 * MIB),
    )(valid, queries, own, other, values)


def combine_kernel(rows_ref, part_ref, out_ref):
    out_ref[...] = jnp.zeros_like(out_ref)
    band_count = out_ref.shape[0]
    sources = part_ref.shape[0]
    for slot in range(SLOTS):
        row = rows_ref[slot]

        @pl.when(row < band_count)
        def _():
            stats = [
                part_ref[i, slot, Q_ROWS:SLOT_ROWS, :].astype(jnp.float32) for i in range(sources)
            ]
            for j, (first, size) in enumerate(((0, HALF), (HALF, QUART))):
                lses = [s[3 * j : 3 * j + 1] + s[3 * j + 1 : 3 * j + 2] + s[3 * j + 2 : 3 * j + 3] for s in stats]
                top = lses[0]
                for lse in lses[1:]:
                    top = jnp.maximum(top, lse)
                shares = [jnp.exp2(lse - top) for lse in lses]
                whole = shares[0]
                for share in shares[1:]:
                    whole = whole + share
                total = jnp.zeros((size, DEPTH), jnp.float32)
                for i in range(sources):
                    share = jnp.broadcast_to(shares[i] / whole, (DEPTH, DEPTH))
                    total = total + jnp.transpose(share)[0:size] * part_ref[
                        i, slot, first : first + size, :
                    ].astype(jnp.float32)
                out_ref[row, first : first + size, :] = total.astype(jnp.bfloat16)


def combine(listed_rows, partials, band_count):
    return pl.pallas_call(
        combine_kernel,
        in_specs=[smem(), vmem()],
        out_specs=vmem(),
        out_shape=jax.ShapeDtypeStruct((band_count, Q_ROWS, DEPTH), jnp.bfloat16),
        compiler_params=pltpu.CompilerParams(vmem_limit_bytes=24 * MIB),
    )(listed_rows, partials)


def unpack_kernel(in_ref, out_ref):
    for chip in range(in_ref.shape[0]):
        trio, second = chip // 2, chip % 2
        head = 3 * trio + 2 * second
        source = jnp.bitwise_xor(chip, flip())
        out_ref[:, head * DEPTH : (head + 1) * DEPTH] = in_ref[source, 0, 0:HALF, :]
        shared = slice((3 * trio + 1) * DEPTH, (3 * trio + 2) * DEPTH)
        out_ref[second * QUART : (second + 1) * QUART, shared] = in_ref[source, 0, HALF:Q_ROWS, :]


def unpack(received, features):
    chips = received.shape[0] // 2
    return pl.pallas_call(
        unpack_kernel,
        grid=(2,),
        in_specs=[pl.BlockSpec((chips, 1, Q_ROWS, DEPTH), lambda core: (0, core, 0, 0))],
        out_specs=pl.BlockSpec((HALF, features), lambda core: (core, 0)),
        out_shape=jax.ShapeDtypeStruct((TOKS, features), jnp.bfloat16),
        cost_estimate=cost(0, 2 * 786432),
    )(received.reshape(chips, 2, Q_ROWS, DEPTH))


def per_device(kv_cache, fresh_qkv, edit_list):
    tile_edge, tile_width, _, features = kv_cache.shape
    band_count = lax.axis_size(ROW)
    col_count = lax.axis_size("col")
    listed_rows = edit_list[:, 0]
    fresh = fresh_qkv.transpose(0, 2, 1, 3)
    chips = lax.axis_size(CHIP)
    query_message = pack_query(fresh, chips)
    got_query = lax.all_to_all(query_message, ROW, 0, 0, tiled=True)
    fresh, query_message = lax.optimization_barrier((fresh, query_message))
    message = pack(listed_rows, kv_cache, fresh)
    picked = pick(listed_rows, got_query)
    message, picked = lax.optimization_barrier((message, picked))
    own = lax.all_to_all(message, ROW, 0, 0, tiled=True)
    pieces = [picked] + [shift(picked, step) for step in range(1, col_count)]
    pieces, own = lax.optimization_barrier((pieces, own))
    queries = join(pieces)
    other = lax.ppermute(own, "core", [(0, 1), (1, 0)])
    queries = queries.reshape(col_count * SLOTS, SLOT_ROWS, DEPTH)
    valid = queries[:, Q_ROWS, 0].astype(jnp.int32)

    partials = attend(valid, queries, own, other, widen(own, other))
    partials = partials.reshape(col_count, SLOTS, SLOT_ROWS, DEPTH)
    partials = across(partials)
    finished = combine(listed_rows, partials, band_count)
    finished = lax.all_to_all(finished, ROW, 0, 0, tiled=True)
    return unpack(finished, features).reshape(tile_edge, tile_width, features)


def solution(mesh):
    rows, cols = mesh.devices.shape
    fine = Mesh(mesh.devices.reshape(rows // 4, 2, 2, cols), ROW + ("col",))
    placed = (P(ROW, "col", None, None), P(ROW, "col", None, None), P(None, "col"))
    return jax.shard_map(
        per_device, mesh=fine, in_specs=placed, out_specs=P(ROW, "col", None), check_vma=False
    )
```

```python
import math

import jax
import jax.numpy as jnp
from jax import lax
from jax.experimental import pallas as pl
from jax.experimental.pallas import tpu as pltpu
from jax.sharding import Mesh, PartitionSpec as P

DEPTH = 128
SLOTS = 4
TOKS = 256
HALF = 128
QUART = 64
KV_ROWS = 4 * HALF
Q_ROWS = HALF + QUART
SLOT_ROWS = Q_ROWS + 16
GROUP = 8
KEY_BLOCK = 512
MIB = 1024 * 1024


def vmem():
    return pl.BlockSpec(memory_space=pltpu.VMEM)


def smem():
    return pl.BlockSpec(memory_space=pltpu.SMEM)


CHIP = ("y", "z_lo")
ROW = CHIP + ("core",)


def flip():
    return lax.axis_index("col") // (lax.axis_size("col") // 2)


def shift(x, step):
    cols = lax.axis_size("col")
    far = step // (cols // 2)
    pairs = [(i, i ^ (far * cols + step)) for i in range(2 * cols)]
    return lax.ppermute(x, ("z_lo", "col"), pairs)


def across(x):
    cols = lax.axis_size("col")
    near, far = list(range(cols // 2)), list(range(cols // 2, cols))
    groups = [near + [cols + i for i in far], [cols + i for i in near] + far]
    return lax.all_to_all(x, ("z_lo", "col"), 0, 0, axis_index_groups=groups, tiled=True)


def cost(flops, moved):
    return pl.CostEstimate(flops=flops, bytes_accessed=moved, transcendentals=0)


def pack_query_kernel(in_ref, out_ref):
    for chip in range(out_ref.shape[0]):
        trio, second = chip // 2, chip % 2
        head = 3 * trio + 2 * second
        dest = jnp.bitwise_xor(chip, flip())
        out_ref[dest, 0, 0:HALF, :] = in_ref[:, 0, :, head * DEPTH : (head + 1) * DEPTH].reshape(
            HALF, DEPTH
        )
        shared = slice((3 * trio + 1) * DEPTH, (3 * trio + 2) * DEPTH)
        rows = slice(second * 4, second * 4 + 4)
        out_ref[dest, 0, HALF:Q_ROWS, :] = in_ref[rows, 0, :, shared].reshape(QUART, DEPTH)


def pack_query(fresh, chips):
    features = fresh.shape[3]
    out = pl.pallas_call(
        pack_query_kernel,
        grid=(2,),
        in_specs=[pl.BlockSpec((8, 1, 16, features), lambda core: (core, 0, 0, 0))],
        out_specs=pl.BlockSpec((chips, 1, Q_ROWS, DEPTH), lambda core: (0, core, 0, 0)),
        out_shape=jax.ShapeDtypeStruct((chips, 2, Q_ROWS, DEPTH), jnp.bfloat16),
        cost_estimate=cost(0, 2 * 786432),
    )(fresh)
    return out.reshape(2 * chips, Q_ROWS, DEPTH)


def fresh_spec(part):
    return pl.BlockSpec((16, 1, 16, 3 * DEPTH), lambda p: (0, part, 0, p))


def pack_kernel(rows_ref, cache_ref, keys_ref, values_ref, out_ref, sorted_ref):
    my_row = lax.axis_index(ROW)
    edited = rows_ref[0] == my_row
    for slot in range(1, SLOTS):
        edited = jnp.logical_or(edited, rows_ref[slot] == my_row)

    @pl.when(edited)
    def _():
        for part, ref in enumerate((keys_ref, values_ref)):
            sorted_ref[part] = ref[...].reshape(TOKS, 3 * DEPTH)

    @pl.when(jnp.logical_not(edited))
    def _():
        place_id = lax.broadcasted_iota(jnp.int32, (TOKS, TOKS), 0)
        source_id = lax.broadcasted_iota(jnp.int32, (TOKS, TOKS), 1)
        wanted = jnp.where(place_id < HALF, 2 * place_id, 2 * place_id - (TOKS - 1))
        sorter = (source_id == wanted).astype(jnp.float32).astype(jnp.bfloat16)
        for half in range(2):
            pairs = cache_ref[half * 8 : half * 8 + 8].reshape(TOKS, 3 * DEPTH)
            apart = jnp.dot(sorter, pairs, preferred_element_type=jnp.float32)
            apart = apart.astype(jnp.bfloat16)
            for part in range(2):
                sorted_ref[part, half * HALF : (half + 1) * HALF, :] = apart[
                    part * HALF : (part + 1) * HALF
                ]

    for chip in range(2):
        dest = jnp.bitwise_xor(chip, flip())
        for core in range(2):
            toks = slice(core * HALF, (core + 1) * HALF)
            for i, head in enumerate((2 * chip, 1)):
                cols = slice(head * DEPTH, (head + 1) * DEPTH)
                for part in range(2):
                    first = (2 * i + part) * HALF
                    out_ref[2 * dest + core, first : first + HALF, :] = sorted_ref[part, toks, cols]


def pack(listed_rows, cache, fresh):
    return pl.pallas_call(
        pack_kernel,
        grid=(4,),
        in_specs=[
            smem(),
            pl.BlockSpec((16, 16, 2, 3 * DEPTH), lambda p: (0, 0, 0, p)),
            fresh_spec(1),
            fresh_spec(2),
        ],
        out_specs=pl.BlockSpec((4, KV_ROWS, DEPTH), lambda p: (p, 0, 0)),
        out_shape=jax.ShapeDtypeStruct((16, KV_ROWS, DEPTH), jnp.bfloat16),
        scratch_shapes=[pltpu.VMEM((2, TOKS, 3 * DEPTH), jnp.bfloat16)],
        cost_estimate=cost(0, 7 * 786432),
        compiler_params=pltpu.CompilerParams(vmem_limit_bytes=20 * MIB),
    )(listed_rows, cache, fresh, fresh)


def join_kernel(*refs):
    for i, ref in enumerate(refs[:-1]):
        refs[-1][i] = ref[...]


def join(pieces):
    return pl.pallas_call(
        join_kernel,
        in_specs=[vmem()] * len(pieces),
        out_specs=vmem(),
        out_shape=jax.ShapeDtypeStruct((len(pieces),) + pieces[0].shape, jnp.bfloat16),
        cost_estimate=cost(0, 4 * MIB),
        compiler_params=pltpu.CompilerParams(vmem_limit_bytes=8 * MIB),
    )(*pieces)


def pick_kernel(rows_ref, got_ref, out_ref):
    bands = got_ref.shape[0]
    for slot in range(SLOTS):
        row = rows_ref[slot]
        rows = got_ref[jnp.minimum(row, bands - 1)]
        flag = jnp.where(row < bands, 1.0, 0.0)
        flags = jnp.full((SLOT_ROWS - Q_ROWS, DEPTH), flag, jnp.float32).astype(jnp.bfloat16)
        out_ref[slot, 0:Q_ROWS, :] = rows
        out_ref[slot, Q_ROWS:SLOT_ROWS, :] = flags


def pick(listed_rows, received):
    return pl.pallas_call(
        pick_kernel,
        in_specs=[smem(), vmem()],
        out_specs=vmem(),
        out_shape=jax.ShapeDtypeStruct((SLOTS, SLOT_ROWS, DEPTH), jnp.bfloat16),
        cost_estimate=cost(0, 2 * 212992),
        compiler_params=pltpu.CompilerParams(vmem_limit_bytes=16 * MIB),
    )(listed_rows, received)


def widen_kernel(own_ref, other_ref, out_ref):
    for head in range(2):
        first = 2 * HALF * head + HALF
        for part, kv_ref in enumerate((own_ref, other_ref)):
            rows = slice(part * 2048, (part + 1) * 2048)
            out_ref[head, rows, 0:DEPTH] = kv_ref[:, first : first + HALF, :].reshape(2048, DEPTH)
        out_ref[head, :, DEPTH:] = jnp.ones((4096, DEPTH), jnp.bfloat16)


def widen(own, other):
    return pl.pallas_call(
        widen_kernel,
        in_specs=[vmem(), vmem()],
        out_specs=vmem(),
        out_shape=jax.ShapeDtypeStruct((2, 4096, 2 * DEPTH), jnp.bfloat16),
        cost_estimate=cost(0, 8 * MIB),
        compiler_params=pltpu.CompilerParams(vmem_limit_bytes=16 * MIB),
    )(own, other)


def attend_rows(queries, kv_refs, values_ref, head):
    fold = math.log2(math.e) / math.sqrt(DEPTH)
    row_max = acc = None
    tiles = KEY_BLOCK // HALF
    first = 2 * HALF * head
    for part, kv_ref in enumerate(kv_refs):
        for block in range(kv_ref.shape[0] // tiles):
            rows = slice(block * tiles, (block + 1) * tiles)
            keys = kv_ref[rows, first : first + HALF, :].reshape(KEY_BLOCK, DEPTH)
            scores = lax.dot_general(
                queries, keys, (((1,), (1,)), ((), ())), preferred_element_type=jnp.float32
            )
            scores = scores * fold
            block_max = jnp.max(scores, axis=1, keepdims=True)
            new_max = block_max if row_max is None else jnp.maximum(row_max, block_max)
            weights = jnp.exp2(scores - new_max).astype(jnp.bfloat16)
            start = part * 2048 + block * KEY_BLOCK
            term = jnp.dot(
                weights,
                values_ref[head, start : start + KEY_BLOCK, :],
                preferred_element_type=jnp.float32,
            )
            if row_max is None:
                acc = term
            else:
                acc = acc * jnp.exp2(row_max - new_max) + term
            row_max = new_max
    total = acc[:, DEPTH:]
    return (acc[:, :DEPTH] / total).astype(jnp.bfloat16), jnp.log2(total) + row_max


def attend_kernel(valid_ref, q_ref, own_ref, other_ref, values_ref, out_ref, table):
    slots = q_ref.shape[0]

    def note(slot, count):
        is_valid = valid_ref[slot]

        @pl.when(is_valid == 1)
        def _():
            table[count] = slot

        return count + is_valid

    count = lax.fori_loop(0, slots, note, jnp.int32(0))
    for extra in range(GROUP):
        table[count + extra] = table[0]

    kv_refs = (own_ref, other_ref)

    def attend_tiles(start, size):
        picks = [table[start + i] for i in range(size)]
        full = jnp.concatenate([q_ref[pick, 0:HALF, :] for pick in picks], axis=0)
        out_full, lse_full = attend_rows(full, kv_refs, values_ref, 0)
        shared = jnp.concatenate([q_ref[pick, HALF:Q_ROWS, :] for pick in picks], axis=0)
        out_shared, lse_shared = attend_rows(shared, kv_refs, values_ref, 1)
        row_ids = lax.broadcasted_iota(jnp.int32, (16, DEPTH), 0)
        picks = [jnp.bitwise_xor(pick, SLOTS * lax.axis_index("col")) for pick in picks]
        for i, pick in enumerate(picks):
            out_ref[pick, 0:HALF, :] = out_full[i * HALF : (i + 1) * HALF]
            out_ref[pick, HALF:Q_ROWS, :] = out_shared[i * QUART : (i + 1) * QUART]
            lse_one = lse_shared[i * QUART : (i + 1) * QUART]
            pair = (
                jnp.transpose(lse_full[i * HALF : (i + 1) * HALF]),
                jnp.transpose(jnp.concatenate([lse_one, lse_one], axis=0)),
            )
            stats = jnp.zeros((16, DEPTH), jnp.float32)
            for j, lanes in enumerate(pair):
                rest = lanes[0:16]
                for term in range(3):
                    piece = rest.astype(jnp.bfloat16).astype(jnp.float32)
                    rest = rest - piece
                    stats = jnp.where(row_ids == 3 * j + term, piece, stats)
            out_ref[pick, Q_ROWS:SLOT_ROWS, :] = stats.astype(jnp.bfloat16)

    eights = (count + 1) // GROUP
    left = count - eights * GROUP

    def body(group, carry):
        attend_tiles(group * GROUP, GROUP)
        return carry

    lax.fori_loop(0, eights, body, 0)
    fours = (left + 1) // 4

    @pl.when(fours > 0)
    def _():
        attend_tiles(eights * GROUP, 4)

    @pl.when(left > 4 * fours)
    def _():
        attend_tiles(eights * GROUP + 4 * fours, 2)


def attend(valid, queries, own, other, values):
    slots = queries.shape[0]
    return pl.pallas_call(
        attend_kernel,
        in_specs=[smem(), vmem(), vmem(), vmem(), vmem()],
        out_specs=vmem(),
        out_shape=jax.ShapeDtypeStruct((slots, SLOT_ROWS, DEPTH), jnp.bfloat16),
        scratch_shapes=[pltpu.SMEM((slots + GROUP,), jnp.int32)],
        cost_estimate=cost(20 * 10**9, 8 * MIB),
        compiler_params=pltpu.CompilerParams(vmem_limit_bytes=30 * MIB),
    )(valid, queries, own, other, values)


def combine_kernel(rows_ref, part_ref, out_ref):
    out_ref[...] = jnp.zeros_like(out_ref)
    band_count = out_ref.shape[0]
    sources = part_ref.shape[0]
    for slot in range(SLOTS):
        row = rows_ref[slot]

        @pl.when(row < band_count)
        def _():
            stats = [
                part_ref[i, slot, Q_ROWS:SLOT_ROWS, :].astype(jnp.float32) for i in range(sources)
            ]
            for j, (first, size) in enumerate(((0, HALF), (HALF, QUART))):
                lses = [s[3 * j : 3 * j + 1] + s[3 * j + 1 : 3 * j + 2] + s[3 * j + 2 : 3 * j + 3] for s in stats]
                top = lses[0]
                for lse in lses[1:]:
                    top = jnp.maximum(top, lse)
                shares = [jnp.exp2(lse - top) for lse in lses]
                whole = shares[0]
                for share in shares[1:]:
                    whole = whole + share
                total = jnp.zeros((size, DEPTH), jnp.float32)
                for i in range(sources):
                    share = jnp.broadcast_to(shares[i] / whole, (DEPTH, DEPTH))
                    total = total + jnp.transpose(share)[0:size] * part_ref[
                        i, slot, first : first + size, :
                    ].astype(jnp.float32)
                out_ref[row, first : first + size, :] = total.astype(jnp.bfloat16)


def combine(listed_rows, partials, band_count):
    return pl.pallas_call(
        combine_kernel,
        in_specs=[smem(), vmem()],
        out_specs=vmem(),
        out_shape=jax.ShapeDtypeStruct((band_count, Q_ROWS, DEPTH), jnp.bfloat16),
        compiler_params=pltpu.CompilerParams(vmem_limit_bytes=24 * MIB),
    )(listed_rows, partials)


def unpack_kernel(in_ref, out_ref):
    for chip in range(in_ref.shape[0]):
        trio, second = chip // 2, chip % 2
        head = 3 * trio + 2 * second
        source = jnp.bitwise_xor(chip, flip())
        out_ref[:, head * DEPTH : (head + 1) * DEPTH] = in_ref[source, 0, 0:HALF, :]
        shared = slice((3 * trio + 1) * DEPTH, (3 * trio + 2) * DEPTH)
        out_ref[second * QUART : (second + 1) * QUART, shared] = in_ref[source, 0, HALF:Q_ROWS, :]


def unpack(received, features):
    chips = received.shape[0] // 2
    return pl.pallas_call(
        unpack_kernel,
        grid=(2,),
        in_specs=[pl.BlockSpec((chips, 1, Q_ROWS, DEPTH), lambda core: (0, core, 0, 0))],
        out_specs=pl.BlockSpec((HALF, features), lambda core: (core, 0)),
        out_shape=jax.ShapeDtypeStruct((TOKS, features), jnp.bfloat16),
        cost_estimate=cost(0, 2 * 786432),
    )(received.reshape(chips, 2, Q_ROWS, DEPTH))


def per_device(kv_cache, fresh_qkv, edit_list):
    tile_edge, tile_width, _, features = kv_cache.shape
    band_count = lax.axis_size(ROW)
    col_count = lax.axis_size("col")
    listed_rows = edit_list[:, 0]
    fresh = fresh_qkv.transpose(0, 2, 1, 3)
    chips = lax.axis_size(CHIP)
    query_message = pack_query(fresh, chips)
    got_query = lax.all_to_all(query_message, ROW, 0, 0, tiled=True)
    fresh, query_message = lax.optimization_barrier((fresh, query_message))
    message = pack(listed_rows, kv_cache, fresh)
    picked = pick(listed_rows, got_query)
    message, picked = lax.optimization_barrier((message, picked))
    own = lax.all_to_all(message, ROW, 0, 0, tiled=True)
    pieces = [picked] + [shift(picked, step) for step in range(1, col_count)]
    pieces, own = lax.optimization_barrier((pieces, own))
    queries = join(pieces)
    other = lax.ppermute(own, "core", [(0, 1), (1, 0)])
    queries = queries.reshape(col_count * SLOTS, SLOT_ROWS, DEPTH)
    valid = queries[:, Q_ROWS, 0].astype(jnp.int32)

    partials = attend(valid, queries, own, other, widen(own, other))
    partials = partials.reshape(col_count, SLOTS, SLOT_ROWS, DEPTH)
    partials = across(partials)
    finished = combine(listed_rows, partials, band_count)
    finished = lax.all_to_all(finished, ROW, 0, 0, tiled=True)
    return unpack(finished, features).reshape(tile_edge, tile_width, features)


def solution(mesh):
    rows, cols = mesh.devices.shape
    fine = Mesh(mesh.devices.reshape(rows // 4, 2, 2, cols), ROW + ("col",))
    placed = (P(ROW, "col", None, None), P(ROW, "col", None, None), P(None, "col"))
    return jax.shard_map(
        per_device, mesh=fine, in_specs=placed, out_specs=P(ROW, "col", None), check_vma=False
    )
```

```python
import math

import jax
import jax.numpy as jnp
from jax import lax
from jax.experimental import pallas as pl
from jax.experimental.pallas import tpu as pltpu
from jax.sharding import Mesh, PartitionSpec as P

DEPTH = 128
SLOTS = 4
TOKS = 256
HALF = 128
QUART = 64
KV_ROWS = 4 * HALF
Q_ROWS = HALF + QUART
SLOT_ROWS = Q_ROWS + 16
FLAG_ROWS = 16
GROUP = 8
KEY_BLOCK = 512
MIB = 1024 * 1024


def vmem():
    return pl.BlockSpec(memory_space=pltpu.VMEM)


def smem():
    return pl.BlockSpec(memory_space=pltpu.SMEM)


CHIP = ("y", "z_lo")
ROW = CHIP + ("core",)


def flip():
    return lax.axis_index("col") // (lax.axis_size("col") // 2)


def shift(x, step):
    cols = lax.axis_size("col")
    far = step // (cols // 2)
    pairs = [(i, i ^ (far * cols + step)) for i in range(2 * cols)]
    return lax.ppermute(x, ("z_lo", "col"), pairs)


def across(x):
    cols = lax.axis_size("col")
    near, far = list(range(cols // 2)), list(range(cols // 2, cols))
    groups = [near + [cols + i for i in far], [cols + i for i in near] + far]
    return lax.all_to_all(x, ("z_lo", "col"), 0, 0, axis_index_groups=groups, tiled=True)


def cost(flops, moved):
    return pl.CostEstimate(flops=flops, bytes_accessed=moved, transcendentals=0)


def pack_query_kernel(in_ref, out_ref):
    for chip in range(out_ref.shape[0]):
        trio, second = chip // 2, chip % 2
        head = 3 * trio + 2 * second
        dest = jnp.bitwise_xor(chip, flip())
        out_ref[dest, 0, 0:HALF, :] = in_ref[:, 0, :, head * DEPTH : (head + 1) * DEPTH].reshape(
            HALF, DEPTH
        )
        shared = slice((3 * trio + 1) * DEPTH, (3 * trio + 2) * DEPTH)
        rows = slice(second * 4, second * 4 + 4)
        out_ref[dest, 0, HALF:Q_ROWS, :] = in_ref[rows, 0, :, shared].reshape(QUART, DEPTH)


def pack_query(fresh, chips):
    features = fresh.shape[3]
    out = pl.pallas_call(
        pack_query_kernel,
        grid=(2,),
        in_specs=[pl.BlockSpec((8, 1, 16, features), lambda core: (core, 0, 0, 0))],
        out_specs=pl.BlockSpec((chips, 1, Q_ROWS, DEPTH), lambda core: (0, core, 0, 0)),
        out_shape=jax.ShapeDtypeStruct((chips, 2, Q_ROWS, DEPTH), jnp.bfloat16),
        cost_estimate=cost(0, 2 * 786432),
    )(fresh)
    return out.reshape(2 * chips, Q_ROWS, DEPTH)


def fresh_spec(part):
    return pl.BlockSpec((16, 1, 16, 3 * DEPTH), lambda p: (0, part, 0, p))


def pack_kernel(rows_ref, cache_ref, keys_ref, values_ref, out_ref, sorted_ref):
    my_row = lax.axis_index(ROW)
    edited = rows_ref[0] == my_row
    for slot in range(1, SLOTS):
        edited = jnp.logical_or(edited, rows_ref[slot] == my_row)

    @pl.when(edited)
    def _():
        for part, ref in enumerate((keys_ref, values_ref)):
            sorted_ref[part] = ref[...].reshape(TOKS, 3 * DEPTH)

    @pl.when(jnp.logical_not(edited))
    def _():
        place_id = lax.broadcasted_iota(jnp.int32, (TOKS, TOKS), 0)
        source_id = lax.broadcasted_iota(jnp.int32, (TOKS, TOKS), 1)
        wanted = jnp.where(place_id < HALF, 2 * place_id, 2 * place_id - (TOKS - 1))
        sorter = (source_id == wanted).astype(jnp.float32).astype(jnp.bfloat16)
        for half in range(2):
            pairs = cache_ref[half * 8 : half * 8 + 8].reshape(TOKS, 3 * DEPTH)
            apart = jnp.dot(sorter, pairs, preferred_element_type=jnp.float32)
            apart = apart.astype(jnp.bfloat16)
            for part in range(2):
                sorted_ref[part, half * HALF : (half + 1) * HALF, :] = apart[
                    part * HALF : (part + 1) * HALF
                ]

    for chip in range(2):
        dest = jnp.bitwise_xor(chip, flip())
        for core in range(2):
            toks = slice(core * HALF, (core + 1) * HALF)
            for i, head in enumerate((2 * chip, 1)):
                cols = slice(head * DEPTH, (head + 1) * DEPTH)
                for part in range(2):
                    first = (2 * i + part) * HALF
                    out_ref[2 * dest + core, first : first + HALF, :] = sorted_ref[part, toks, cols]


def pack(listed_rows, cache, fresh):
    return pl.pallas_call(
        pack_kernel,
        grid=(4,),
        in_specs=[
            smem(),
            pl.BlockSpec((16, 16, 2, 3 * DEPTH), lambda p: (0, 0, 0, p)),
            fresh_spec(1),
            fresh_spec(2),
        ],
        out_specs=pl.BlockSpec((4, KV_ROWS, DEPTH), lambda p: (p, 0, 0)),
        out_shape=jax.ShapeDtypeStruct((16, KV_ROWS, DEPTH), jnp.bfloat16),
        scratch_shapes=[pltpu.VMEM((2, TOKS, 3 * DEPTH), jnp.bfloat16)],
        cost_estimate=cost(0, 7 * 786432),
        compiler_params=pltpu.CompilerParams(vmem_limit_bytes=20 * MIB),
    )(listed_rows, cache, fresh, fresh)


def join_kernel(*refs):
    for i, ref in enumerate(refs[:-1]):
        refs[-1][i] = ref[...]


def join(pieces):
    return pl.pallas_call(
        join_kernel,
        in_specs=[vmem()] * len(pieces),
        out_specs=vmem(),
        out_shape=jax.ShapeDtypeStruct((len(pieces),) + pieces[0].shape, jnp.bfloat16),
        cost_estimate=cost(0, 4 * MIB),
        compiler_params=pltpu.CompilerParams(vmem_limit_bytes=8 * MIB),
    )(*pieces)


def pick_kernel(rows_ref, got_ref, out_ref):
    bands = got_ref.shape[0]
    row_ids = lax.broadcasted_iota(jnp.int32, (FLAG_ROWS, DEPTH), 0)
    flags = jnp.zeros((FLAG_ROWS, DEPTH), jnp.float32)
    for slot in range(SLOTS):
        row = rows_ref[slot]
        out_ref[slot * Q_ROWS : (slot + 1) * Q_ROWS, :] = got_ref[jnp.minimum(row, bands - 1)]
        flags = jnp.where(row_ids == slot, jnp.where(row < bands, 1.0, 0.0), flags)
    out_ref[SLOTS * Q_ROWS :, :] = flags.astype(jnp.bfloat16)


def pick(listed_rows, received):
    return pl.pallas_call(
        pick_kernel,
        in_specs=[smem(), vmem()],
        out_specs=vmem(),
        out_shape=jax.ShapeDtypeStruct((SLOTS * Q_ROWS + FLAG_ROWS, DEPTH), jnp.bfloat16),
        cost_estimate=cost(0, 2 * 200704),
        compiler_params=pltpu.CompilerParams(vmem_limit_bytes=16 * MIB),
    )(listed_rows, received)


def widen_kernel(own_ref, other_ref, out_ref):
    for head in range(2):
        first = 2 * HALF * head + HALF
        for part, kv_ref in enumerate((own_ref, other_ref)):
            rows = slice(part * 2048, (part + 1) * 2048)
            out_ref[head, rows, 0:DEPTH] = kv_ref[:, first : first + HALF, :].reshape(2048, DEPTH)
        out_ref[head, :, DEPTH:] = jnp.ones((4096, DEPTH), jnp.bfloat16)


def widen(own, other):
    return pl.pallas_call(
        widen_kernel,
        in_specs=[vmem(), vmem()],
        out_specs=vmem(),
        out_shape=jax.ShapeDtypeStruct((2, 4096, 2 * DEPTH), jnp.bfloat16),
        cost_estimate=cost(0, 8 * MIB),
        compiler_params=pltpu.CompilerParams(vmem_limit_bytes=16 * MIB),
    )(own, other)


def attend_rows(queries, kv_refs, values_ref, head):
    fold = math.log2(math.e) / math.sqrt(DEPTH)
    row_max = acc = None
    tiles = KEY_BLOCK // HALF
    first = 2 * HALF * head
    for part, kv_ref in enumerate(kv_refs):
        for block in range(kv_ref.shape[0] // tiles):
            rows = slice(block * tiles, (block + 1) * tiles)
            keys = kv_ref[rows, first : first + HALF, :].reshape(KEY_BLOCK, DEPTH)
            scores = lax.dot_general(
                queries, keys, (((1,), (1,)), ((), ())), preferred_element_type=jnp.float32
            )
            scores = scores * fold
            block_max = jnp.max(scores, axis=1, keepdims=True)
            new_max = block_max if row_max is None else jnp.maximum(row_max, block_max)
            weights = jnp.exp2(scores - new_max).astype(jnp.bfloat16)
            start = part * 2048 + block * KEY_BLOCK
            term = jnp.dot(
                weights,
                values_ref[head, start : start + KEY_BLOCK, :],
                preferred_element_type=jnp.float32,
            )
            if row_max is None:
                acc = term
            else:
                acc = acc * jnp.exp2(row_max - new_max) + term
            row_max = new_max
    total = acc[:, DEPTH:]
    return (acc[:, :DEPTH] / total).astype(jnp.bfloat16), jnp.log2(total) + row_max


def attend_kernel(valid_ref, q_ref, own_ref, other_ref, values_ref, out_ref, table):
    slots = q_ref.shape[0] * SLOTS

    def note(slot, count):
        is_valid = valid_ref[slot]

        @pl.when(is_valid == 1)
        def _():
            table[count] = slot

        return count + is_valid

    count = lax.fori_loop(0, slots, note, jnp.int32(0))
    for extra in range(GROUP):
        table[count + extra] = table[0]

    kv_refs = (own_ref, other_ref)

    def attend_tiles(start, size):
        picks = [table[start + i] for i in range(size)]
        starts = [pl.multiple_of(pick % SLOTS * Q_ROWS, QUART) for pick in picks]
        full = jnp.concatenate(
            [q_ref[pick // SLOTS, pl.ds(at, HALF), :] for pick, at in zip(picks, starts)], axis=0
        )
        out_full, lse_full = attend_rows(full, kv_refs, values_ref, 0)
        shared = jnp.concatenate(
            [q_ref[pick // SLOTS, pl.ds(at + HALF, QUART), :] for pick, at in zip(picks, starts)],
            axis=0,
        )
        out_shared, lse_shared = attend_rows(shared, kv_refs, values_ref, 1)
        row_ids = lax.broadcasted_iota(jnp.int32, (16, DEPTH), 0)
        picks = [jnp.bitwise_xor(pick, SLOTS * lax.axis_index("col")) for pick in picks]
        for i, pick in enumerate(picks):
            out_ref[pick, 0:HALF, :] = out_full[i * HALF : (i + 1) * HALF]
            out_ref[pick, HALF:Q_ROWS, :] = out_shared[i * QUART : (i + 1) * QUART]
            lse_one = lse_shared[i * QUART : (i + 1) * QUART]
            pair = (
                jnp.transpose(lse_full[i * HALF : (i + 1) * HALF]),
                jnp.transpose(jnp.concatenate([lse_one, lse_one], axis=0)),
            )
            stats = jnp.zeros((16, DEPTH), jnp.float32)
            for j, lanes in enumerate(pair):
                rest = lanes[0:16]
                for term in range(3):
                    piece = rest.astype(jnp.bfloat16).astype(jnp.float32)
                    rest = rest - piece
                    stats = jnp.where(row_ids == 3 * j + term, piece, stats)
            out_ref[pick, Q_ROWS:SLOT_ROWS, :] = stats.astype(jnp.bfloat16)

    eights = (count + 1) // GROUP
    left = count - eights * GROUP

    def body(group, carry):
        attend_tiles(group * GROUP, GROUP)
        return carry

    lax.fori_loop(0, eights, body, 0)
    fours = (left + 1) // 4

    @pl.when(fours > 0)
    def _():
        attend_tiles(eights * GROUP, 4)

    @pl.when(left > 4 * fours)
    def _():
        attend_tiles(eights * GROUP + 4 * fours, 2)


def attend(valid, queries, own, other, values):
    slots = queries.shape[0] * SLOTS
    return pl.pallas_call(
        attend_kernel,
        in_specs=[smem(), vmem(), vmem(), vmem(), vmem()],
        out_specs=vmem(),
        out_shape=jax.ShapeDtypeStruct((slots, SLOT_ROWS, DEPTH), jnp.bfloat16),
        scratch_shapes=[pltpu.SMEM((slots + GROUP,), jnp.int32)],
        cost_estimate=cost(20 * 10**9, 8 * MIB),
        compiler_params=pltpu.CompilerParams(vmem_limit_bytes=30 * MIB),
    )(valid, queries, own, other, values)


def combine_kernel(rows_ref, part_ref, out_ref):
    out_ref[...] = jnp.zeros_like(out_ref)
    band_count = out_ref.shape[0]
    sources = part_ref.shape[0]
    for slot in range(SLOTS):
        row = rows_ref[slot]

        @pl.when(row < band_count)
        def _():
            stats = [
                part_ref[i, slot, Q_ROWS:SLOT_ROWS, :].astype(jnp.float32) for i in range(sources)
            ]
            for j, (first, size) in enumerate(((0, HALF), (HALF, QUART))):
                lses = [s[3 * j : 3 * j + 1] + s[3 * j + 1 : 3 * j + 2] + s[3 * j + 2 : 3 * j + 3] for s in stats]
                top = lses[0]
                for lse in lses[1:]:
                    top = jnp.maximum(top, lse)
                shares = [jnp.exp2(lse - top) for lse in lses]
                whole = shares[0]
                for share in shares[1:]:
                    whole = whole + share
                total = jnp.zeros((size, DEPTH), jnp.float32)
                for i in range(sources):
                    share = jnp.broadcast_to(shares[i] / whole, (DEPTH, DEPTH))
                    total = total + jnp.transpose(share)[0:size] * part_ref[
                        i, slot, first : first + size, :
                    ].astype(jnp.float32)
                out_ref[row, first : first + size, :] = total.astype(jnp.bfloat16)


def combine(listed_rows, partials, band_count):
    return pl.pallas_call(
        combine_kernel,
        in_specs=[smem(), vmem()],
        out_specs=vmem(),
        out_shape=jax.ShapeDtypeStruct((band_count, Q_ROWS, DEPTH), jnp.bfloat16),
        compiler_params=pltpu.CompilerParams(vmem_limit_bytes=24 * MIB),
    )(listed_rows, partials)


def unpack_kernel(in_ref, out_ref):
    for chip in range(in_ref.shape[0]):
        trio, second = chip // 2, chip % 2
        head = 3 * trio + 2 * second
        source = jnp.bitwise_xor(chip, flip())
        out_ref[:, head * DEPTH : (head + 1) * DEPTH] = in_ref[source, 0, 0:HALF, :]
        shared = slice((3 * trio + 1) * DEPTH, (3 * trio + 2) * DEPTH)
        out_ref[second * QUART : (second + 1) * QUART, shared] = in_ref[source, 0, HALF:Q_ROWS, :]


def unpack(received, features):
    chips = received.shape[0] // 2
    return pl.pallas_call(
        unpack_kernel,
        grid=(2,),
        in_specs=[pl.BlockSpec((chips, 1, Q_ROWS, DEPTH), lambda core: (0, core, 0, 0))],
        out_specs=pl.BlockSpec((HALF, features), lambda core: (core, 0)),
        out_shape=jax.ShapeDtypeStruct((TOKS, features), jnp.bfloat16),
        cost_estimate=cost(0, 2 * 786432),
    )(received.reshape(chips, 2, Q_ROWS, DEPTH))


def per_device(kv_cache, fresh_qkv, edit_list):
    tile_edge, tile_width, _, features = kv_cache.shape
    band_count = lax.axis_size(ROW)
    col_count = lax.axis_size("col")
    listed_rows = edit_list[:, 0]
    fresh = fresh_qkv.transpose(0, 2, 1, 3)
    chips = lax.axis_size(CHIP)
    query_message = pack_query(fresh, chips)
    got_query = lax.all_to_all(query_message, ROW, 0, 0, tiled=True)
    fresh, query_message = lax.optimization_barrier((fresh, query_message))
    message = pack(listed_rows, kv_cache, fresh)
    picked = pick(listed_rows, got_query)
    message, picked = lax.optimization_barrier((message, picked))
    own = lax.all_to_all(message, ROW, 0, 0, tiled=True)
    pieces = [picked] + [shift(picked, step) for step in range(1, col_count)]
    pieces, own = lax.optimization_barrier((pieces, own))
    queries = join(pieces)
    other = lax.ppermute(own, "core", [(0, 1), (1, 0)])
    flags = queries[:, SLOTS * Q_ROWS : SLOTS * Q_ROWS + SLOTS, 0]
    valid = flags.reshape(col_count * SLOTS).astype(jnp.int32)

    partials = attend(valid, queries, own, other, widen(own, other))
    partials = partials.reshape(col_count, SLOTS, SLOT_ROWS, DEPTH)
    partials = across(partials)
    finished = combine(listed_rows, partials, band_count)
    finished = lax.all_to_all(finished, ROW, 0, 0, tiled=True)
    return unpack(finished, features).reshape(tile_edge, tile_width, features)


def solution(mesh):
    rows, cols = mesh.devices.shape
    fine = Mesh(mesh.devices.reshape(rows // 4, 2, 2, cols), ROW + ("col",))
    placed = (P(ROW, "col", None, None), P(ROW, "col", None, None), P(None, "col"))
    return jax.shard_map(
        per_device, mesh=fine, in_specs=placed, out_specs=P(ROW, "col", None), check_vma=False
    )
```
